128 devices in a mesh: grp: 4 (over y), dev: 32 (over x, z, core).
Axes of the slice: x: 4, y: 4, z: 4, core: 2. Of those that a mesh axis runs over, the one named last changes fastest.
Arguments:
- iterate: float32 [216, 131072], P(None, ('grp', 'dev')), may hold values from -6 to 6
- rhs: float32 [216, 131072], P(None, ('grp', 'dev')), may hold values from -12 to 12
- material: float32 [2, 131072], P(None, ('grp', 'dev')), may hold values from 0.25 to 4
- orders: int32 [131072], P(('grp', 'dev')), may hold values from 0 to 4
- new_owner: int32 [131072, 1], P(('grp', 'dev')), may hold values from 0 to 127; in each aligned block of 1024 rows (0 to 1023, 1024 to 2047, ...) at most 16 rows name the same one
- face_send: int32 [2, 65536], P(None, ('grp', 'dev')), may hold values from 0 to 40959
- face_recv: int32 [2, 65536], P(None, ('grp', 'dev')), may hold values from 0 to 40959
- face_flip: int32 [2, 65536], P(None, ('grp', 'dev')), may hold values from 0 to 1
- stiff_off: float32 [5, 216, 216], replicated, may hold values from -0.4375 to 0.4375
- stiff_diag: float32 [5, 216], replicated, may hold values from 1.5 to 3
- mass_diag: float32 [5, 216], replicated, may hold values from 0.25 to 2
Outputs:
- new_iterate: float32 [216, 262144], P(None, ('grp', 'dev'))
- residual: float32 [216, 262144], P(None, ('grp', 'dev'))
The draws below stay inside these ranges and needn't reach their ends.
Inputs may be any that keep to these rules, and one draw needn't show every extreme that they name: `new_owner`: of one device's 1024 elements at most 16 have the same new owner, and exactly 16 share one for some owner. `face_send`: A row r names dof r // 2048 of slot r % 2048. `face_recv`: A row r names dof r // 2048 of slot r % 2048; rows may repeat.
All inputs are finite; a program needn't handle non-finite values.
Results may differ from the reference program's by a relative error of at most 0.0003.
Values sent between devices are 32-bit elements; how exact they have to be, the bound alone decides.
No kernel may reach another device: no remote copies, remote signals or barrier semaphores. Data moves between devices by JAX's collectives and lax.ppermute only.
A program may use at most 128 MiB of HBM per device.

```python
import math
import jax
import jax.numpy as jnp
import numpy as np
from jax import lax

NB = 216
ORDERS = 5
FACE_DOFS = 20
E_DEV = 1024
FACE_DEV = 512
OWNERS = 128
CAP = 16
RECV = 2048
ELEMS = 131072
FACES = 65536
TOTAL = 262144
N_DEV = 32


def touch_ends(values, own_key, least, top_value):
    shape = values.shape
    place = [jax.random.randint(jax.random.fold_in(own_key, axis), (), 0, shape[axis]) for axis in range(len(shape))]
    values = values.at[tuple(place)].set(least)
    longest = shape.index(max(shape))
    place[longest] = (place[longest] + 1) % shape[longest]
    return values.at[tuple(place)].set(top_value)


def shard_levels(own_key, dims, split, smallest, top_value):
    level = 1.0
    for axis_at, shards_of in split:
        heights = jax.random.uniform(jax.random.fold_in(jax.random.fold_in(own_key, 6), axis_at), (shards_of,), jnp.float32, smallest / len(split), top_value / len(split))
        level = level * jnp.repeat(jnp.exp(heights), dims[axis_at] // shards_of).reshape((-1,) + (1,) * (len(dims) - 1 - axis_at))
    return level


def shared_out(rng, own, number, rows, count, top, reach, slope):
    order = jax.random.permutation(rng, count)
    packed, ordinary = load_shares(count, rows * top, reach, slope, True), load_shares(count, rows * top, reach, slope, False)
    places = jnp.arange(count)

    def named(lengths, offset_by):
        used = int((lengths > 0).sum())
        fixed = max(1, used // 4)
        passed = fixed + (places - fixed + offset_by * (used - fixed)) % max(1, count - fixed)
        return jnp.zeros((count,), jnp.int32).at[order[jnp.where(places < fixed, places, passed)]].set(jnp.asarray(lengths, jnp.int32))

    lengths = jnp.where(number % 4 == 0, named(packed, number // 4), named(ordinary, number - number // 4 - 1))
    mixed = jax.random.permutation(jax.random.fold_in(own, 3), count)
    donor, taker = mixed[0:count // 2 * 2:2], mixed[1:count // 2 * 2:2]
    slack = jnp.minimum(lengths[donor] - 1, reach - lengths[taker]) // 2
    slack = jnp.where((donor == order[0]) | (taker == order[0]) | (lengths[taker] == 0), 0, jnp.maximum(slack, 0))
    passed = jax.random.randint(jax.random.fold_in(own, 4), (count // 2,), 0, 1 << 20) % (slack + 1)
    lengths = lengths.at[donor].add(-passed).at[taker].add(passed)
    items = jnp.searchsorted(jnp.cumsum(lengths), jnp.arange(rows * top), side="right").astype(jnp.int32)
    grid = items.reshape(top, rows).T
    grid = grid[jax.random.permutation(jax.random.fold_in(own, 1), rows)]
    offset_by = jax.random.randint(jax.random.fold_in(own, 2), (rows, 1), 0, top)
    return jnp.take_along_axis(grid, (jnp.arange(top)[None, :] + offset_by) % top, axis=1)


def load_shares(number_of, total, reach, slope, full):
    loads = [(1 << 20) // math.isqrt(rank ** slope) + 1 for rank in range(1, number_of + 1)]
    largest = reach if full else min(reach, max(-(-total // number_of), total * loads[0] // sum(loads)))
    least = 1 if total - largest >= number_of - 1 else 0
    given, surplus = [largest] + [least] * (number_of - 1), total - largest - least * (number_of - 1)
    while surplus > 0:
        movable = [i for i in range(1, number_of) if given[i] < largest] or [i for i in range(1, number_of) if given[i] < reach]
        whole, budget = sum([loads[i] for i in movable]), surplus
        for i in movable:
            more = min(reach - given[i], max(1, budget * loads[i] // whole), surplus)
            given[i] = given[i] + more
            surplus = surplus - more
    return np.array(given)


def scatter_about(key, extent, spread, bound, pieces=(), held_as=jnp.bfloat16):
    entries = jax.random.normal(key, extent, jnp.float32) * spread
    if len(pieces) > 0:
        entries = shard_levels(key, extent, pieces, -0.22, 0.18) * entries
    return jnp.clip(entries, min=-bound, max=bound).astype(held_as)


def setup_inputs(seed: int = 0) -> dict:
    streams_of = jax.random.split(jax.random.key(seed), 12)
    iterate = scatter_about(streams_of[0], (NB, ELEMS), 1.0, 6.0, ((1, 128),), jnp.float32)
    rhs = scatter_about(streams_of[1], (NB, ELEMS), 2.0, 12.0, ((1, 128),), jnp.float32)
    material = jnp.clip(jnp.exp(math.log(4.0) - 2.7725887 * jax.random.uniform(streams_of[2], (2, ELEMS), jnp.float32) ** shard_levels(streams_of[2], (2, ELEMS), ((1, 128),), -0.2, 0.2)), 0.25, 4.0)
    orders = touch_ends(jax.random.randint(streams_of[3], (ELEMS,), 0, ORDERS), jax.random.fold_in(streams_of[3], 1), 0, ORDERS - 1).astype(jnp.int32)
    new_owner_keys = jax.random.split(jax.random.fold_in(streams_of[4], 1), ELEMS // E_DEV)
    new_owner_turns = jax.random.permutation(jax.random.fold_in(streams_of[4], 3), ELEMS // E_DEV)
    new_owner = jax.vmap(lambda own, number: shared_out(jax.random.fold_in(streams_of[4], 2), own, number, E_DEV, OWNERS, 1, CAP, 2))(new_owner_keys, new_owner_turns).reshape((ELEMS, 1))
    face_send = touch_ends(jax.random.randint(streams_of[5], (2, FACES), 0, FACE_DOFS * RECV), jax.random.fold_in(streams_of[5], 1), 0, (FACE_DOFS * RECV) - 1).astype(jnp.int32)
    face_recv = touch_ends(jax.random.randint(streams_of[6], (2, FACES), 0, FACE_DOFS * RECV), jax.random.fold_in(streams_of[6], 1), 0, (FACE_DOFS * RECV) - 1).astype(jnp.int32)
    face_flip = touch_ends(jax.random.randint(streams_of[7], (2, FACES), 0, 2), jax.random.fold_in(streams_of[7], 1), 0, 1).astype(jnp.int32)
    stiff_off = scatter_about(streams_of[8], (ORDERS, NB, NB), NB ** -0.5, 0.4375, (), jnp.float32)
    stiff_diag = jnp.clip(jax.random.uniform(streams_of[9], (ORDERS, NB), jnp.float32, 1.5, 3.0), 1.5, 3.0)
    mass_diag = jnp.clip(jnp.exp(jax.random.uniform(streams_of[10], (ORDERS, NB), jnp.float32, math.log(0.25), math.log(2.0))), 0.25, 2.0)
    return {"iterate": iterate, "rhs": rhs, "material": material, "orders": orders, "new_owner": new_owner, "face_send": face_send, "face_recv": face_recv, "face_flip": face_flip, "stiff_off": stiff_off, "stiff_diag": stiff_diag, "mass_diag": mass_diag}


cheby_weight = 2.0 / (2.0 + 0.2)


def dof_count(order_index, dof_width):
    order_value = order_index + 2
    return min(dof_width, order_value * (order_value + 2) * (order_value + 3) // 2)


def fill_slots(values, target, owners, slot_cap):
    matches = (target[:, None] == jnp.arange(owners, dtype=jnp.int32)[None, :]).astype(jnp.int32)
    earlier = jnp.sum(jnp.cumsum(matches, axis=0) * matches, axis=1) - 1
    slots_at = (target * slot_cap + earlier).astype(jnp.int32)
    blank_buffer = jnp.zeros((values.shape[0], owners * slot_cap), values.dtype)
    return blank_buffer.at[:, slots_at].set(values)


def migrate(values, new_owner):
    dof_rows = values.shape[0]
    by_source = values.reshape(dof_rows, OWNERS, E_DEV).transpose(1, 0, 2)
    targets = new_owner[:, 0].reshape(OWNERS, E_DEV)

    def one_source(source_block, target):
        return fill_slots(source_block, target, OWNERS, CAP)

    sent = jax.vmap(one_source)(by_source, targets)
    sent = sent.reshape(OWNERS, dof_rows, OWNERS, CAP)
    return sent.transpose(1, 2, 0, 3).reshape(dof_rows, OWNERS * OWNERS * CAP)


def element_terms(reluctance, mass_coef, order_index, occupied, stiff_diag, mass_diag, dof_width):
    dof_rows = jnp.arange(dof_width, dtype=jnp.int32)[:, None]
    divisor = jnp.ones((dof_width, reluctance.shape[0]), jnp.float32)
    selections = []
    for k in range(stiff_diag.shape[0]):
        selected = (dof_rows < dof_count(k, dof_width)) & ((order_index == k) & occupied)[None, :]
        diag_value = reluctance[None, :] * stiff_diag[k][:, None] + mass_coef[None, :] * mass_diag[k][:, None]
        divisor = jnp.where(selected, diag_value, divisor)
        selections.append(selected)
    live_rows = selections[0]
    for selected in selections[1:]:
        live_rows = live_rows | selected
    return divisor, selections, live_rows


def apply_block(field_dofs, reluctance, mass_coef, order_index, occupied, stiff_off, stiff_diag, mass_diag):
    dof_width = field_dofs.shape[0]
    divisor, selections, live_rows = element_terms(reluctance, mass_coef, order_index, occupied, stiff_diag, mass_diag, dof_width)
    summed = jnp.zeros(field_dofs.shape, jnp.float32)
    for k in range(len(selections)):
        masked = jnp.where(selections[k], field_dofs, 0.0)
        product = jnp.dot(stiff_off[k], masked, precision=lax.Precision.HIGHEST, preferred_element_type=jnp.float32)
        element_term = reluctance[None, :] * (product + stiff_diag[k][:, None] * masked) + mass_coef[None, :] * mass_diag[k][:, None] * masked
        summed = summed + jnp.where(selections[k], element_term, 0.0)
    return summed, divisor, live_rows


def add_faces(flat_rows, recv_up, values_up, recv_down, values_down):
    return flat_rows.at[recv_up].add(values_up).at[recv_down].add(values_down)


def reference(iterate, rhs, material, orders, new_owner, face_send, face_recv, face_flip, stiff_off, stiff_diag, mass_diag):
    field_dofs = migrate(iterate, new_owner)
    source = migrate(rhs, new_owner)
    coef_rows = migrate(material, new_owner)
    order_index = migrate(orders[None, :], new_owner)[0]
    occupied = coef_rows[0] > 0.0
    applied, divisor, live_rows = apply_block(field_dofs, coef_rows[0], coef_rows[1], order_index, occupied, stiff_off, stiff_diag, mass_diag)
    flat_rows = applied.reshape(NB, OWNERS, RECV).transpose(1, 0, 2).reshape(OWNERS, NB * RECV)
    send_lists = face_send.reshape(2, OWNERS, FACE_DEV)
    recv_lists = face_recv.reshape(2, OWNERS, FACE_DEV)
    face_signs = (1 - 2 * face_flip).astype(jnp.float32).reshape(2, OWNERS, FACE_DEV)
    up_values = jnp.take_along_axis(flat_rows, send_lists[0], axis=1)
    down_values = jnp.take_along_axis(flat_rows, send_lists[1], axis=1)
    in_group = jnp.arange(OWNERS, dtype=jnp.int32) % N_DEV
    nothing = jnp.zeros((1, FACE_DEV), jnp.float32)
    from_below = jnp.concatenate([nothing, up_values[:-1]], axis=0)
    from_below = jnp.where((in_group > 0)[:, None], from_below, 0.0)
    from_above = jnp.concatenate([down_values[1:], nothing], axis=0)
    from_above = jnp.where((in_group < N_DEV - 1)[:, None], from_above, 0.0)
    flat_rows = jax.vmap(add_faces)(flat_rows, recv_lists[0], face_signs[0] * from_below, recv_lists[1], face_signs[1] * from_above)
    summed = flat_rows.reshape(OWNERS, NB, RECV).transpose(1, 0, 2).reshape(NB, TOTAL)
    residual = jnp.where(live_rows, source - summed, 0.0)
    new_iterate = jnp.where(live_rows, field_dofs + cheby_weight * residual / divisor, 0.0)
    return new_iterate, residual
```

```python
import functools

import jax
import jax.numpy as jnp
from jax import lax
from jax.experimental import pallas as pl
from jax.experimental.pallas import tpu as pltpu
from jax.sharding import PartitionSpec as P

F32 = jnp.float32
BF16 = jnp.bfloat16
CHEBY = 2.0 / (2.0 + 0.2)
DOFS = 216
LIVE = (20, 45, 84, 140, 216)
PADDED = (24, 48, 88, 144, 216)
HEAD = 24
BODY = DOFS - HEAD
CAP = 16
ROWS = 56
COEFS = 16
HEAD_ROWS = 8 * HEAD + COEFS
BODY_OFF = sum(n - HEAD for n in PADDED[1:])
BODY_ROWS = BODY_OFF + BODY
NT = (((1,), (1,)), ((), ()))
MIB = 1 << 20


def swapped(array, axis, first):
    devices = lax.axis_size(axis)
    lower = range(first, devices - 1, 2)
    return lax.ppermute(array, axis, [p for i in lower for p in ((i, i + 1), (i + 1, i))])


def two_pieces(x):
    hi = x.astype(BF16)
    return hi, (x - hi.astype(F32)).astype(BF16)


def dot(a, b, dims=(((1,), (0,)), ((), ()))):
    return lax.dot_general(a, b, dims, preferred_element_type=F32)


def coefficients(material, order):
    c0, c1 = material[0:1], material[1:2]
    live = jnp.zeros(order.shape, jnp.int32)
    for k, n in enumerate(LIVE):
        live = jnp.where(order == k, n, live)
    rows = [c0, c1, live.astype(F32), jnp.zeros(order.shape, F32)]
    for c in (c0, c1):
        rows += [jnp.where(order == k, c, 0.0) for k in range(len(LIVE))]
    rows += [jnp.zeros(order.shape, F32)] * (COEFS - len(rows))
    return jnp.concatenate(rows, axis=0)


def ranks_of(own_row, owners):
    chunk = 128
    upper = (
        lax.broadcasted_iota(jnp.int32, (chunk, chunk), 0)
        < lax.broadcasted_iota(jnp.int32, (chunk, chunk), 1)
    )
    sums = jnp.concatenate([upper.astype(F32), jnp.ones((chunk, chunk), F32)], axis=1).astype(BF16)
    carry = jnp.zeros((owners, chunk), F32)
    ranks = []
    for c in range(own_row.shape[1] // chunk):
        named = (
            lax.broadcasted_iota(jnp.int32, (owners, chunk), 0)
            == own_row[:, c * chunk : (c + 1) * chunk]
        ).astype(F32)
        both = dot(named.astype(BF16), sums)
        earlier = both[:, :chunk] + carry
        carry = carry + both[:, chunk:]
        ranks.append(jnp.sum(named * earlier, axis=0, keepdims=True))
    return jnp.concatenate(ranks, axis=1).astype(jnp.int32)


def weights_of(off, diag_t, mass_t):
    lanes = lax.broadcasted_iota(jnp.int32, (DOFS, 256), 1)
    pad = jnp.zeros((DOFS, 256 - DOFS), F32)
    blocks = []
    for k, n in enumerate(LIVE):
        blocks.append(jnp.where(lanes < n, jnp.concatenate([off[k], pad], axis=1), 0.0))
    divisor = jnp.concatenate([jnp.zeros((DOFS, 128), F32), diag_t + mass_t], axis=1)

    def units(rows, start):
        place = lax.broadcasted_iota(jnp.int32, (rows, 256), 0) + start
        return (place == lax.broadcasted_iota(jnp.int32, (rows, 256), 1)).astype(F32)

    head = jnp.concatenate(
        [b[:HEAD] for b in blocks]
        + [divisor[:HEAD], units(HEAD, 0), units(HEAD, DOFS), units(COEFS, 256 - COEFS)],
        axis=0,
    )
    body = jnp.concatenate(
        [b[HEAD:n] for b, n in zip(blocks[1:], PADDED[1:])] + [divisor[HEAD:]], axis=0
    )
    return head, body


def three_passes(w):
    hi, lo = two_pieces(w)
    return jnp.concatenate([hi, lo, hi], axis=1)


def side_by_side(pair, swap):
    both = pair[...]
    there, back = (jnp.concatenate([both[i : i + 1], both[1 - i : 2 - i]], axis=1) for i in (0, 1))
    return jnp.where(swap, back, there)


def odd_device():
    return lax.rem(lax.axis_index("dev"), 2) == 1


def pack_kernel(
    field_in, source_in, material_in, orders_in, owner_in, off_in, diag_in, mass_in, at_in, flip_in,
    out, head_out, body_out, rows_out, lanes_out,
    field, source, material, orders, owner, off, diag, mass, at, flip,
    head_w, body_w, rows_of, lanes_of,
    t0, t1, t2, t3, b0, b1, b2, b3, b4, table, index, placed, in_sems, out_sems, sem,
):
    count = field.shape[1]
    owners = out.shape[0]
    chunk = 128
    loads = []
    for src, dst in (
        (owner_in, owner),
        (field_in, field),
        (source_in, source),
        (orders_in, orders),
        (material_in, material),
        (off_in, off),
        (diag_in, diag),
        (mass_in, mass),
        (at_in, at),
        (flip_in, flip),
    ):
        loads.append(pltpu.make_async_copy(src, dst, in_sems.at[len(loads)]))
        loads[-1].start()
    sends = []

    def send(src, dst):
        sends.append(pltpu.make_async_copy(src, dst, out_sems.at[len(sends)]))
        sends[-1].start()

    b1[...] = jnp.zeros(b1.shape, F32)
    table[...] = jnp.zeros(table.shape, F32)
    loads[0].wait()
    own_row = owner[...]
    index[...] = own_row * CAP + ranks_of(own_row, owners)
    copy = pltpu.make_async_copy(index, placed, sem)
    copy.start()
    for c in loads[1:]:
        c.wait()

    coefs = coefficients(material[...], orders[...])
    for c in range(count // chunk):
        here = slice(c * chunk, (c + 1) * chunk)
        t0[here, :] = field[0:128, here].T
        t1[here, :] = jnp.concatenate(
            [field[128:DOFS, here], source[0:HEAD, here], coefs[:, here]], axis=0
        ).T
        t2[here, :] = source[HEAD : HEAD + 128, here].T
        tail = source[HEAD + 128 : DOFS, here]
        t3[here, :] = jnp.concatenate([tail, tail], axis=0).T

    first = 256 - COEFS + 4 - 128
    orders_held = len(LIVE)
    table[0, first : first + orders_held, 0:DOFS] = diag[...]
    table[1, first + orders_held : first + 2 * orders_held, 0:DOFS] = mass[...]
    head, body = weights_of(off, table[0].T[:DOFS], table[1].T[:DOFS])
    head_w[...] = three_passes(head)
    body_w[...] = three_passes(body)
    swap = jnp.logical_not(odd_device())
    row = side_by_side(at, swap)
    signs = (1 - 2 * side_by_side(flip, swap)).astype(F32)
    faces = row.shape[1]
    mine = lax.broadcasted_iota(jnp.int32, (HEAD * 16, faces), 0) == row // 128
    rows_of[...] = mine.astype(F32).astype(BF16)
    spot = lax.broadcasted_iota(jnp.int32, (128, faces), 0) == lax.rem(row, 128)
    lanes_of[...] = jnp.where(spot, signs, 0.0)
    copy.wait()
    for src, dst in (
        (head_w, head_out),
        (body_w, body_out),
        (rows_of, rows_out),
        (lanes_of, lanes_out),
    ):
        send(src, dst)

    def place(pairs):
        def step(g, carry):
            for j in range(16):
                i = g * 16 + j
                slot = placed[0, i]
                for rows, block in pairs:
                    block[pl.ds(slot, 1), :] = rows[pl.ds(i, 1), :]
            return carry

        lax.fori_loop(0, count // 16, step, 0)

    def send_rows(block, start, size):
        send(block.reshape(owners, size, 128), out.at[:, start : start + size, :])

    place([(t0, b0), (t1, b1)])
    send_rows(b0, 0, CAP)
    send_rows(b1, CAP, CAP)
    place([(t2, b2), (t3, b3)])
    send_rows(b2, 2 * CAP, CAP)
    halves = b3[...].reshape(owners, CAP, 128)
    low = lax.broadcasted_iota(jnp.int32, (owners, CAP // 2, 128), 2) < 64
    b4[...] = jnp.where(low, halves[:, 0 : CAP // 2], halves[:, CAP // 2 :]).reshape(b4.shape)
    send_rows(b4, 3 * CAP, CAP // 2)
    for c in sends:
        c.wait()


def pack(operands, owners):
    count = operands[0].shape[1]
    faces = 2 * operands[-1].shape[1]
    hbm = pl.BlockSpec(memory_space=pltpu.HBM)
    made = [
        jax.ShapeDtypeStruct((HEAD_ROWS, 768), BF16),
        jax.ShapeDtypeStruct((BODY_ROWS, 768), BF16),
        jax.ShapeDtypeStruct((HEAD * 16, faces), BF16),
        jax.ShapeDtypeStruct((128, faces), F32),
    ]
    return pl.pallas_call(
        pack_kernel,
        out_shape=[jax.ShapeDtypeStruct((owners, ROWS, 128), F32)] + made,
        in_specs=[hbm] * len(operands),
        out_specs=[hbm] * 5,
        scratch_shapes=[pltpu.VMEM(a.shape, a.dtype) for a in list(operands) + made]
        + [pltpu.VMEM((count, 128), F32)] * 4
        + [pltpu.VMEM((owners * CAP, 128), F32)] * 4
        + [
            pltpu.VMEM((owners * CAP // 2, 128), F32),
            pltpu.VMEM((2, 128, 256), F32),
            pltpu.VMEM((1, count), jnp.int32),
            pltpu.SMEM((1, count), jnp.int32),
            pltpu.SemaphoreType.DMA((len(operands),)),
            pltpu.SemaphoreType.DMA((8,)),
            pltpu.SemaphoreType.DMA,
        ],
        compiler_params=pltpu.CompilerParams(vmem_limit_bytes=60 * MIB),
        name="pack",
    )(*operands)


def slot_pieces(x0, x1):
    hi, lo = two_pieces(jnp.concatenate([x0, x1], axis=1))
    return jnp.concatenate([hi, hi, lo], axis=1)


def head_kernel(recv, w, send, base, field, step, one, two, applied_at, *, group):
    slots = group * CAP
    for t in range(recv.shape[0] // group):
        at = slice(t * group, (t + 1) * group)
        x0 = recv[at, 0:CAP, :].reshape(-1, 128)
        x1 = recv[at, CAP : 2 * CAP, :].reshape(-1, 128)
        y = dot(w[...], slot_pieces(x0, x1), NT)
        diag, x, rhs = (y[(5 + i) * HEAD : (6 + i) * HEAD] for i in range(3))
        coefs = y[8 * HEAD :]
        c0, live = coefs[0:1], coefs[2:3]
        product = y[0:HEAD]
        for k in range(1, len(LIVE)):
            product = jnp.where(coefs[4 + k : 5 + k] > 0.0, y[k * HEAD : (k + 1) * HEAD], product)
        rows = lax.broadcasted_iota(jnp.int32, (HEAD, slots), 0).astype(F32)
        alive = rows + 0.5 < live
        divisor = jnp.where(alive, diag, 1.0)
        applied = jnp.where(alive, c0 * product + divisor * x, 0.0)
        here = slice(t * slots, (t + 1) * slots)
        applied_at[:, here] = applied
        base[:, here] = jnp.where(alive, rhs - applied, 0.0)
        field[:, here] = jnp.where(alive, x, 0.0)
        step[:, here] = jnp.where(alive, CHEBY / divisor, 0.0)

    row = side_by_side(send, odd_device())
    slot = lax.rem(row, 2048)
    lane, block, dof = lax.rem(slot, 128), slot // 128, row // 2048
    rows = lax.broadcasted_iota(jnp.int32, (8, 128), 0)
    for i in range(row.shape[1] // 128):
        part = slice(i * 128, (i + 1) * 128)
        lanes = jnp.broadcast_to(lane[:, part], (8, 128))
        blocks = jnp.broadcast_to(block[:, part], (8, 128))
        dofs = jnp.broadcast_to(dof[:, part], (8, 128))
        total = jnp.zeros((8, 128), F32)
        for d in range(HEAD // 8):
            found = jnp.zeros((8, 128), F32)
            for b in range(applied_at.shape[1] // 128):
                held = applied_at[d * 8 : (d + 1) * 8, b * 128 : (b + 1) * 128]
                taken = jnp.take_along_axis(held, lanes, axis=1, mode="promise_in_bounds")
                found = jnp.where(blocks == b, taken, found)
            total = total + jnp.where(rows + d * 8 == dofs, found, 0.0)
        values = jnp.sum(total, axis=0, keepdims=True)
        if i < 4:
            one[i : i + 1, :] = values
        else:
            two[i - 4 : i - 3, :] = values


def head_rows(recv, w, face_send, group):
    slots = recv.shape[0] * CAP
    vmem = pl.BlockSpec(memory_space=pltpu.VMEM)
    return pl.pallas_call(
        functools.partial(head_kernel, group=group),
        out_shape=[jax.ShapeDtypeStruct((HEAD, slots), F32)] * 3
        + [jax.ShapeDtypeStruct((4, 128), F32)] * 2,
        in_specs=[vmem] * 3,
        out_specs=[vmem] * 5,
        scratch_shapes=[pltpu.VMEM((HEAD, slots), F32)],
        compiler_params=pltpu.CompilerParams(vmem_limit_bytes=24 * MIB),
        cost_estimate=pl.CostEstimate(flops=2 * 10**9, bytes_accessed=4 * 10**6, transcendentals=0),
        name="head_rows",
    )(recv, w, face_send)


def body_kernel(recv, w, fresh, residual):
    x0, x1, x2 = (recv[:, i * CAP : (i + 1) * CAP, :].reshape(-1, 128) for i in range(3))
    slots = x0.shape[0]
    y = dot(w[...], slot_pieces(x0, x1), NT)
    x1t = x1.T
    field = jnp.concatenate([x0.T[HEAD:], x1t[0 : DOFS - 128]], axis=0)
    last = recv[:, 3 * CAP :, :]
    last = jnp.stack([last, pltpu.roll(last.reshape(-1, 128), 64, 1).reshape(last.shape)], axis=1)
    rhs = jnp.concatenate([x2.T, last.reshape(-1, 128).T[0:64]], axis=0)
    coefs = x1t[128 - COEFS :]
    c0, live = coefs[0:1], coefs[2:3]
    product = None
    start = BODY_OFF
    for k in range(len(LIVE) - 1, 0, -1):
        size = PADDED[k] - HEAD
        start -= size
        mine = y[start : start + size]
        if product is None:
            product = mine
        else:
            top = jnp.where(coefs[4 + k : 5 + k] > 0.0, mine, product[0:size])
            product = jnp.concatenate([top, product[size:]], axis=0)
    rows = lax.broadcasted_iota(jnp.int32, (BODY, slots), 0).astype(F32) + HEAD
    alive = rows + 0.5 < live
    divisor = jnp.where(alive, y[BODY_OFF:], 1.0)
    left = jnp.where(alive, rhs - c0 * product - divisor * field, 0.0)
    residual[HEAD:, :] = left
    fresh[HEAD:, :] = jnp.where(alive, field + CHEBY * left / divisor, 0.0)


def body_rows(recv, w, group):
    partners = recv.shape[0]
    slots = partners * CAP
    wide = pl.BlockSpec((DOFS, group * CAP), lambda t: (0, t))
    return pl.pallas_call(
        body_kernel,
        grid=(partners // group,),
        out_shape=[jax.ShapeDtypeStruct((DOFS, slots), F32)] * 2,
        in_specs=[
            pl.BlockSpec((group, ROWS, 128), lambda t: (t, 0, 0)),
            pl.BlockSpec(memory_space=pltpu.VMEM),
        ],
        out_specs=[wide] * 2,
        compiler_params=pltpu.CompilerParams(vmem_limit_bytes=24 * MIB),
        cost_estimate=pl.CostEstimate(flops=4 * 10**9, bytes_accessed=8 * 10**6, transcendentals=0),
        name="body_rows",
    )(recv, w)


def finish_kernel(one, two, rows_of, lanes_of, base, field, step, _, __, fresh, residual, flat):
    values = jnp.concatenate(
        [one[i : i + 1, :] for i in range(4)] + [two[i : i + 1, :] for i in range(4)], axis=1
    )
    hi, mid = (p.astype(F32) for p in two_pieces(values))
    spread = lanes_of[...]
    pieces = jnp.concatenate([spread * hi, spread * mid, spread * (values - hi - mid)], axis=0)
    found = dot(rows_of[...], pieces.astype(BF16), NT)
    flat[...] = found[:, 0:128] + found[:, 128:256] + found[:, 256:384]
    for b in range(16):
        at = slice(b * 128, (b + 1) * 128)
        added = flat[pl.ds(b, HEAD, stride=16), :]
        scale = step[:, at]
        left = jnp.where(scale > 0.0, base[:, at] - added, 0.0)
        residual[:, at] = left
        fresh[:, at] = field[:, at] + scale * left


def finish(one, two, rows_of, lanes_of, base, field, step, fresh, residual):
    vmem = pl.BlockSpec(memory_space=pltpu.VMEM)
    there = pl.BlockSpec(memory_space=pl.ANY)
    first = pl.BlockSpec(base.shape, lambda t: (0, 0))
    return pl.pallas_call(
        finish_kernel,
        grid=(1,),
        out_shape=[jax.ShapeDtypeStruct(fresh.shape, F32)] * 2,
        in_specs=[vmem] * 7 + [there] * 2,
        out_specs=[first] * 2,
        scratch_shapes=[pltpu.VMEM((HEAD * 16, 128), F32)],
        input_output_aliases={7: 0, 8: 1},
        compiler_params=pltpu.CompilerParams(vmem_limit_bytes=24 * MIB),
        cost_estimate=pl.CostEstimate(flops=10**9, bytes_accessed=10**6, transcendentals=0),
        name="finish",
    )(one, two, rows_of, lanes_of, base, field, step, fresh, residual)


def per_device(
    iterate,
    rhs,
    material,
    orders,
    new_owner,
    face_send,
    face_recv,
    face_flip,
    stiff_off,
    stiff_diag,
    mass_diag,
):
    count = iterate.shape[1]
    owners = lax.axis_size("grp") * lax.axis_size("dev")
    packed, head_w, body_w, rows_of, lanes_of = pack(
        (
            iterate,
            rhs,
            material,
            orders.reshape(1, count),
            new_owner.reshape(1, count),
            stiff_off,
            stiff_diag,
            mass_diag,
            face_recv,
            face_flip,
        ),
        owners,
    )
    recv = lax.all_to_all(packed, ("grp", "dev"), split_axis=0, concat_axis=0, tiled=True)
    base, field, step, one, two = head_rows(recv, head_w, face_send, 16)
    one, two = swapped(one, "dev", 0), swapped(two, "dev", 1)
    fresh, residual = body_rows(recv, body_w, 32)
    return finish(one, two, rows_of, lanes_of, base, field, step, fresh, residual)


def solution(mesh):
    both = ("grp", "dev")
    return jax.shard_map(
        per_device,
        mesh=mesh,
        in_specs=(
            P(None, both),
            P(None, both),
            P(None, both),
            P(both),
            P(both, None),
            P(None, both),
            P(None, both),
            P(None, both),
            P(),
            P(),
            P(),
        ),
        out_specs=(P(None, both), P(None, both)),
        check_vma=False,
    )
```

```python
import functools

import jax
import jax.numpy as jnp
from jax import lax
from jax.experimental import pallas as pl
from jax.experimental.pallas import tpu as pltpu
from jax.sharding import PartitionSpec as P

F32 = jnp.float32
BF16 = jnp.bfloat16
CHEBY = 2.0 / (2.0 + 0.2)
DOFS = 216
LIVE = (20, 45, 84, 140, 216)
PADDED = (24, 48, 88, 144, 216)
HEAD = 24
BODY = DOFS - HEAD
CAP = 16
COEFS = 16
NEAR = 88
NEAR_ROWS = CAP + CAP // 2
POOL = 24
POOL_MAX = 2 * CAP
POOL_STRIDE = POOL_MAX + 8
NEAR_W = (len(LIVE) + 3) * HEAD + COEFS
BODY_OFF = sum(n - HEAD for n in PADDED[1:])
BODY_ROWS = BODY_OFF + BODY
NT = (((1,), (1,)), ((), ()))
MIB = 1 << 20


def swapped(array, axis, first):
    devices = lax.axis_size(axis)
    lower = range(first, devices - 1, 2)
    return lax.ppermute(array, axis, [p for i in lower for p in ((i, i + 1), (i + 1, i))])


def two_pieces(x):
    hi = x.astype(BF16)
    return hi, (x - hi.astype(F32)).astype(BF16)


def dot(a, b, dims=(((1,), (0,)), ((), ()))):
    return lax.dot_general(a, b, dims, preferred_element_type=F32)


def coefficients(material, order, first_row, overflow):
    c0, c1 = material[0:1], material[1:2]
    live = jnp.zeros(order.shape, jnp.int32)
    for k, n in enumerate(LIVE):
        live = jnp.where(order == k, n, live)
    rows = [c0, c1, live.astype(F32), first_row]
    for c in (c0, c1):
        rows += [jnp.where(order == k, c, 0.0) for k in range(len(LIVE))]
    rows += [jnp.zeros(order.shape, F32), jnp.broadcast_to(overflow, order.shape)]
    return jnp.concatenate(rows, axis=0)


def ranks_of(own_row, sizes, owners):
    chunk = 128
    upper = (
        lax.broadcasted_iota(jnp.int32, (chunk, chunk), 0)
        < lax.broadcasted_iota(jnp.int32, (chunk, chunk), 1)
    )
    sums = jnp.concatenate([upper.astype(F32), jnp.ones((chunk, chunk), F32)], axis=1).astype(BF16)
    carry = jnp.zeros((2 * owners, chunk), F32)
    ranks, firsts = [], []
    for c in range(own_row.shape[1] // chunk):
        here = slice(c * chunk, (c + 1) * chunk)
        named = (
            lax.broadcasted_iota(jnp.int32, (owners, chunk), 0) == own_row[:, here]
        ).astype(F32)
        marks = jnp.concatenate([named, named * sizes[:, here]], axis=0).astype(BF16)
        both = dot(marks, sums)
        earlier = both[:, :chunk] + carry
        carry = carry + both[:, chunk:]
        ranks.append(jnp.sum(named * earlier[:owners], axis=0, keepdims=True))
        firsts.append(jnp.sum(named * earlier[owners:], axis=0, keepdims=True))
    return (jnp.concatenate(v, axis=1) for v in (ranks, firsts)), jnp.max(carry[owners:])


def weights_of(off, divisor):
    lanes = lax.broadcasted_iota(jnp.int32, (HEAD, 128), 1)

    def units(rows, start):
        place = lax.broadcasted_iota(jnp.int32, (rows, 128), 0) + start
        return (place == lax.broadcasted_iota(jnp.int32, (rows, 128), 1)).astype(F32)

    near = [
        jnp.where(lanes < min(n, NEAR), off[k, 0:HEAD, 0:128], 0.0) for k, n in enumerate(LIVE)
    ]
    near += [pltpu.roll(divisor, 128 - COEFS - (DOFS - 128), 1)[:HEAD]]
    near += [units(HEAD, 0), units(HEAD, NEAR), units(COEFS, 128 - COEFS)]
    pool = [
        jnp.where(lanes < LIVE[k] - NEAR, off[k, 0:HEAD, NEAR:DOFS], 0.0) for k in (4, 3)
    ]
    pad = jnp.zeros((DOFS, 256 - DOFS), F32)
    body = [
        jnp.concatenate([off[k], pad], axis=1)[HEAD:n] for k, n in enumerate(PADDED) if k > 0
    ]
    body += [jnp.concatenate([jnp.zeros((DOFS, 128), F32), divisor], axis=1)[HEAD:]]
    return (jnp.concatenate(v, axis=0) for v in (near, pool, body))


def three_passes(w):
    hi, lo = two_pieces(w)
    return jnp.concatenate([hi, lo, hi], axis=1)


def side_by_side(pair, swap):
    both = pair[...]
    there, back = (jnp.concatenate([both[i : i + 1], both[1 - i : 2 - i]], axis=1) for i in (0, 1))
    return jnp.where(swap, back, there)


def odd_device():
    return lax.rem(lax.axis_index("dev"), 2) == 1


def pack_kernel(
    owner_in, orders_in, at_in, flip_in, material_in, diag_in, mass_in, field_in, source_in, off_in,
    out, extra, near_out, far_out, body_out, rows_out, lanes_out,
    owner, orders, at, flip, material, diag, mass, field, source, off,
    near_w, far_w, body_w, rows_of, lanes_of,
    t0, t1, t2, t3, whole, halves, merged, pool, table,
    slot_index, pool_index, slot_at, pool_at, in_sems, out_sems, index_sems,
):
    count = field.shape[1]
    owners = out.shape[0]
    chunk = 128
    loads = []
    for src, dst in (
        (owner_in, owner),
        (orders_in, orders),
        (at_in, at),
        (flip_in, flip),
        (material_in, material),
        (diag_in, diag),
        (mass_in, mass),
        (field_in, field),
        (source_in, source),
        (off_in, off),
    ):
        loads.append(pltpu.make_async_copy(src, dst, in_sems.at[len(loads)]))
        loads[-1].start()
    sends = []

    def send(src, dst):
        sends.append(pltpu.make_async_copy(src, dst, out_sems.at[len(sends)]))
        sends[-1].start()

    table[...] = jnp.zeros(table.shape, F32)
    for c in loads[0:2]:
        c.wait()
    own_row, order = owner[...], orders[...]
    sizes = jnp.where(order == 4, 2.0, jnp.where(order == 3, 1.0, 0.0))
    (rank, first_row), largest = ranks_of(own_row, sizes, owners)
    slot_index[...] = own_row * CAP + rank.astype(jnp.int32)
    pool_index[...] = own_row * POOL_STRIDE + first_row.astype(jnp.int32)
    copies = [
        pltpu.make_async_copy(src, dst, index_sems.at[i])
        for i, (src, dst) in enumerate(((pool_index, pool_at), (slot_index, slot_at)))
    ]
    for c in copies:
        c.start()
    overflow = jnp.where(largest > POOL, 1.0, 0.0)
    last = lax.broadcasted_iota(jnp.int32, whole.shape, 1) == 127
    whole[...] = jnp.where(last, overflow, 0.0)

    for c in loads[2:7]:
        c.wait()
    swap = jnp.logical_not(odd_device())
    row = side_by_side(at, swap)
    signs = (1 - 2 * side_by_side(flip, swap)).astype(F32)
    faces = row.shape[1]
    mine = lax.broadcasted_iota(jnp.int32, (HEAD * 16, faces), 0) == row // 128
    rows_of[...] = mine.astype(F32).astype(BF16)
    spot = lax.broadcasted_iota(jnp.int32, (128, faces), 0) == lax.rem(row, 128)
    lanes_of[...] = jnp.where(spot, signs, 0.0)
    first = DOFS + 4 - 128
    orders_held = len(LIVE)
    table[first : first + orders_held, 0:DOFS] = diag[...]
    table[first + orders_held : first + 2 * orders_held, 0:DOFS] = mass[...]
    coefs = coefficients(material[...], order, first_row, overflow)

    for c in loads[7:]:
        c.wait()
    for c in range(count // chunk):
        here = slice(c * chunk, (c + 1) * chunk)
        t0[here, :] = jnp.concatenate(
            [field[0:NEAR, here], source[0:HEAD, here], coefs[:, here]], axis=0
        ).T
        middle = source[HEAD:NEAR, here]
        t1[here, :] = jnp.concatenate([middle, middle], axis=0).T
        top = jnp.where(order[:, here] == 4, field[NEAR + 64 : DOFS, here], source[NEAR : NEAR + 64, here])
        t2[here, :] = jnp.concatenate([field[NEAR : NEAR + 64, here], top], axis=0).T
        t3[here, :] = source[NEAR:DOFS, here].T
    near, far, body = weights_of(off, table[...].T[:DOFS])
    near_w[...] = three_passes(near)
    far_w[...] = three_passes(far)
    body_w[...] = three_passes(body)
    for c in copies:
        c.wait()
    for src, dst in (
        (near_w, near_out),
        (far_w, far_out),
        (body_w, body_out),
        (rows_of, rows_out),
        (lanes_of, lanes_out),
    ):
        send(src, dst)

    def place(row_at, steps):
        def step(g, carry):
            for j in range(32):
                i = g * 32 + j
                row = row_at[0, i]
                for rows, block, ahead in steps:
                    block[pl.ds(row + ahead, 1), :] = rows[pl.ds(i, 1), :]
            return carry

        lax.fori_loop(0, count // 32, step, 0)

    place(pool_at, [(t2, pool, 0), (t3, pool, 1)])
    pools = pool.reshape(owners, POOL_STRIDE, 128)
    send(pools.at[:, 0:POOL, :], out.at[:, NEAR_ROWS : NEAR_ROWS + POOL, :])
    send(pools.at[:, POOL:POOL_MAX, :], extra)
    place(slot_at, [(t0, whole, 0), (t1, halves, 0)])
    send(whole.reshape(owners, CAP, 128), out.at[:, 0:CAP, :])
    both = halves[...].reshape(owners, CAP, 128)
    low = lax.broadcasted_iota(jnp.int32, (owners, CAP // 2, 128), 2) < 64
    both = jnp.where(low, both[:, 0 : CAP // 2], both[:, CAP // 2 :])
    merged[...] = both.reshape(merged.shape)
    send(merged.reshape(owners, CAP // 2, 128), out.at[:, CAP:NEAR_ROWS, :])
    for c in sends:
        c.wait()


def pack(operands, owners):
    count = operands[0].shape[1]
    faces = 2 * operands[2].shape[1]
    hbm = pl.BlockSpec(memory_space=pltpu.HBM)
    made = [
        jax.ShapeDtypeStruct((NEAR_W, 384), BF16),
        jax.ShapeDtypeStruct((2 * HEAD, 384), BF16),
        jax.ShapeDtypeStruct((BODY_ROWS, 768), BF16),
        jax.ShapeDtypeStruct((HEAD * 16, faces), BF16),
        jax.ShapeDtypeStruct((128, faces), F32),
    ]
    return pl.pallas_call(
        pack_kernel,
        out_shape=[
            jax.ShapeDtypeStruct((owners, NEAR_ROWS + POOL, 128), F32),
            jax.ShapeDtypeStruct((owners, POOL_MAX - POOL, 128), F32),
        ]
        + made,
        in_specs=[hbm] * len(operands),
        out_specs=[hbm] * 7,
        scratch_shapes=[pltpu.VMEM(a.shape, a.dtype) for a in list(operands) + made]
        + [pltpu.VMEM((count, 128), F32)] * 4
        + [pltpu.VMEM((owners * CAP, 128), F32)] * 2
        + [
            pltpu.VMEM((owners * CAP // 2, 128), F32),
            pltpu.VMEM((owners * POOL_STRIDE, 128), F32),
            pltpu.VMEM((128, 256), F32),
            pltpu.VMEM((1, count), jnp.int32),
            pltpu.VMEM((1, count), jnp.int32),
            pltpu.SMEM((1, count), jnp.int32),
            pltpu.SMEM((1, count), jnp.int32),
            pltpu.SemaphoreType.DMA((len(operands),)),
            pltpu.SemaphoreType.DMA((9,)),
            pltpu.SemaphoreType.DMA((2,)),
        ],
        compiler_params=pltpu.CompilerParams(vmem_limit_bytes=60 * MIB),
        name="pack",
    )(*operands)


def pool_columns(pools, first_row):
    rows, wide = pools.shape
    partners = first_row.shape[1] // CAP
    held = wide // partners
    lane = lax.broadcasted_iota(jnp.int32, (1, 128), 1)
    tiles = []
    for j in range(partners // 8):
        start = j * 8 * held
        tile = start // 128
        at = start % 128 + lane // CAP * held + first_row[:, j * 128 : (j + 1) * 128]
        second = jnp.broadcast_to(at >= 128, (8, 128))
        at = jnp.broadcast_to(jnp.bitwise_and(at, 127), (8, 128))

        def taken(r, tile):
            part = pools[r : r + 8, tile * 128 : (tile + 1) * 128]
            return jnp.take_along_axis(part, at, axis=1, mode="promise_in_bounds")

        tiles.append(
            jnp.concatenate(
                [jnp.where(second, taken(r, tile + 1), taken(r, tile)) for r in range(0, rows, 8)],
                axis=0,
            )
        )
    return jnp.concatenate(tiles, axis=1)


def field_pieces(values):
    wide = values.shape[1]
    full = jnp.concatenate([values, jnp.zeros((256 - values.shape[0], wide), F32)], axis=0)
    hi, lo = two_pieces(full)
    return jnp.concatenate([hi, hi, lo], axis=0)


def flag_kernel(recv, flag, same):
    flags = jnp.max(jnp.max(recv[:, 0:8, :], axis=0), axis=0, keepdims=True)
    last = lax.broadcasted_iota(jnp.int32, flags.shape, 1) == 127
    flag[...] = jnp.max(jnp.where(last, flags, 0.0), axis=1, keepdims=True)
    same[...] = flag[...]


def flag_of(recv):
    vmem = pl.BlockSpec(memory_space=pltpu.VMEM)
    return pl.pallas_call(
        flag_kernel,
        out_shape=[jax.ShapeDtypeStruct((1, 1), F32)] * 2,
        in_specs=[vmem],
        out_specs=[vmem] * 2,
        compiler_params=pltpu.CompilerParams(vmem_limit_bytes=16 * MIB),
        name="flag_of",
    )(recv)


def load_overflow(flag, extra, more, sem):
    @pl.when(jnp.max(flag[...]) > 0.5)
    def _():
        copy = pltpu.make_async_copy(extra, more, sem)
        copy.start()
        copy.wait()


def row_pieces(rows):
    hi, lo = two_pieces(rows)
    return jnp.concatenate([hi, hi, lo], axis=1)


def head_kernel(
    recv, flag, extra, near_w, far_w, send,
    base, field, step, one, two, applied_at, more, sem, *, group,
):
    load_overflow(flag, extra, more, sem)
    slots = group * CAP
    for t in range(recv.shape[0] // group):
        at = slice(t * group, (t + 1) * group)
        here = slice(t * slots, (t + 1) * slots)
        near = recv[at, 0:CAP, :].reshape(-1, 128)
        pools = jnp.concatenate([recv[at, NEAR_ROWS:, :], more[at]], axis=1).reshape(-1, 128)
        y = dot(near_w[...], row_pieces(near), NT)
        z = dot(far_w[...], row_pieces(pools), NT)
        diag, x, rhs = (y[(5 + i) * HEAD : (6 + i) * HEAD] for i in range(3))
        coefs = y[8 * HEAD :]
        c0, live = coefs[0:1], coefs[2:3]
        far = pool_columns(z, (coefs[3:4] + 0.5).astype(jnp.int32))
        product = y[0:HEAD]
        for k in range(1, len(LIVE)):
            mine = y[k * HEAD : (k + 1) * HEAD]
            if k >= 3:
                mine = mine + far[(4 - k) * HEAD : (5 - k) * HEAD]
            product = jnp.where(coefs[4 + k : 5 + k] > 0.0, mine, product)
        rows = lax.broadcasted_iota(jnp.int32, (HEAD, slots), 0).astype(F32)
        alive = rows + 0.5 < live
        divisor = jnp.where(alive, diag, 1.0)
        applied = jnp.where(alive, c0 * product + divisor * x, 0.0)
        applied_at[:, here] = applied
        base[:, here] = jnp.where(alive, rhs - applied, 0.0)
        field[:, here] = jnp.where(alive, x, 0.0)
        step[:, here] = jnp.where(alive, CHEBY / divisor, 0.0)

    row = side_by_side(send, odd_device())
    slot = lax.rem(row, 2048)
    lane, block, dof = lax.rem(slot, 128), slot // 128, row // 2048
    rows = lax.broadcasted_iota(jnp.int32, (8, 128), 0)
    for i in range(row.shape[1] // 128):
        part = slice(i * 128, (i + 1) * 128)
        lanes = jnp.broadcast_to(lane[:, part], (8, 128))
        blocks = jnp.broadcast_to(block[:, part], (8, 128))
        dofs = jnp.broadcast_to(dof[:, part], (8, 128))
        total = jnp.zeros((8, 128), F32)
        for d in range(HEAD // 8):
            found = jnp.zeros((8, 128), F32)
            for b in range(applied_at.shape[1] // 128):
                held = applied_at[d * 8 : (d + 1) * 8, b * 128 : (b + 1) * 128]
                taken = jnp.take_along_axis(held, lanes, axis=1, mode="promise_in_bounds")
                found = jnp.where(blocks == b, taken, found)
            total = total + jnp.where(rows + d * 8 == dofs, found, 0.0)
        values = jnp.sum(total, axis=0, keepdims=True)
        if i < 4:
            one[i : i + 1, :] = values
        else:
            two[i - 4 : i - 3, :] = values


def head_rows(recv, flag, extra, near_w, far_w, face_send, group):
    slots = recv.shape[0] * CAP
    vmem = pl.BlockSpec(memory_space=pltpu.VMEM)
    there = pl.BlockSpec(memory_space=pltpu.HBM)
    return pl.pallas_call(
        functools.partial(head_kernel, group=group),
        out_shape=[jax.ShapeDtypeStruct((HEAD, slots), F32)] * 3
        + [jax.ShapeDtypeStruct((4, 128), F32)] * 2,
        in_specs=[vmem] * 2 + [there] + [vmem] * 3,
        out_specs=[vmem] * 5,
        scratch_shapes=[
            pltpu.VMEM((HEAD, slots), F32),
            pltpu.VMEM(extra.shape, F32),
            pltpu.SemaphoreType.DMA,
        ],
        compiler_params=pltpu.CompilerParams(vmem_limit_bytes=24 * MIB),
        cost_estimate=pl.CostEstimate(flops=2 * 10**9, bytes_accessed=4 * 10**6, transcendentals=0),
        name="head_rows",
    )(recv, flag, extra, near_w, far_w, face_send)


def body_kernel(recv, flag, extra, w, fresh, residual, more, sem):
    t = pl.program_id(0)

    @pl.when(t == 0)
    def _():
        load_overflow(flag, extra, more, sem)

    group = recv.shape[0]
    slots = group * CAP
    near = recv[:, 0:CAP, :].reshape(-1, 128).T
    middle = recv[:, CAP:NEAR_ROWS, :]
    turned = pltpu.roll(middle.reshape(-1, 128), 64, 1).reshape(middle.shape)
    middle = jnp.stack([middle, turned], axis=1).reshape(-1, 128).T[0:64]
    rest = more[pl.ds(t * group, group), :, :]
    pools = jnp.concatenate([recv[:, NEAR_ROWS:, :], rest], axis=1).reshape(-1, 128).T
    coefs = near[128 - COEFS :]
    c0, live = coefs[0:1], coefs[2:3]
    first_row = coefs[3:4].astype(jnp.int32)
    far = pool_columns(pools, first_row)
    far_rhs = pool_columns(pools, first_row + 1)
    rows = lax.broadcasted_iota(jnp.int32, (DOFS, slots), 0).astype(F32)
    alive = rows + 0.5 < live
    values = jnp.where(alive, jnp.concatenate([near[0:NEAR], far], axis=0), 0.0)
    y = dot(w[...], field_pieces(jnp.concatenate([values, coefs], axis=0)))
    top = jnp.where(coefs[8:9] > 0.0, far_rhs[0:64], far[64:128])
    rhs = jnp.concatenate([middle, top, far_rhs[64:]], axis=0)
    product = None
    start = BODY_OFF
    for k in range(len(LIVE) - 1, 0, -1):
        size = PADDED[k] - HEAD
        start -= size
        mine = y[start : start + size]
        if product is None:
            product = mine
        else:
            best = jnp.where(coefs[4 + k : 5 + k] > 0.0, mine, product[0:size])
            product = jnp.concatenate([best, product[size:]], axis=0)
    alive = alive[HEAD:]
    field = values[HEAD:]
    divisor = jnp.where(alive, y[BODY_OFF:], 1.0)
    left = jnp.where(alive, rhs - c0 * product - divisor * field, 0.0)
    residual[HEAD:, :] = left
    fresh[HEAD:, :] = field + CHEBY * left / divisor


def body_rows(recv, flag, extra, w, group):
    partners, rows = recv.shape[:2]
    slots = partners * CAP
    vmem = pl.BlockSpec(memory_space=pltpu.VMEM)
    wide = pl.BlockSpec((DOFS, group * CAP), lambda t: (0, t))
    return pl.pallas_call(
        body_kernel,
        grid=(partners // group,),
        out_shape=[jax.ShapeDtypeStruct((DOFS, slots), F32)] * 2,
        in_specs=[
            pl.BlockSpec((group, rows, 128), lambda t: (t, 0, 0)),
            vmem,
            pl.BlockSpec(memory_space=pltpu.HBM),
            vmem,
        ],
        out_specs=[wide] * 2,
        scratch_shapes=[pltpu.VMEM(extra.shape, F32), pltpu.SemaphoreType.DMA],
        compiler_params=pltpu.CompilerParams(vmem_limit_bytes=24 * MIB),
        cost_estimate=pl.CostEstimate(flops=4 * 10**9, bytes_accessed=8 * 10**6, transcendentals=0),
        name="body_rows",
    )(recv, flag, extra, w)


def finish_kernel(one, two, rows_of, lanes_of, base, field, step, _, __, fresh, residual, flat):
    values = jnp.concatenate(
        [one[i : i + 1, :] for i in range(4)] + [two[i : i + 1, :] for i in range(4)], axis=1
    )
    hi, mid = (p.astype(F32) for p in two_pieces(values))
    spread = lanes_of[...]
    pieces = jnp.concatenate([spread * hi, spread * mid, spread * (values - hi - mid)], axis=0)
    found = dot(rows_of[...], pieces.astype(BF16), NT)
    flat[...] = found[:, 0:128] + found[:, 128:256] + found[:, 256:384]
    for b in range(16):
        at = slice(b * 128, (b + 1) * 128)
        added = flat[pl.ds(b, HEAD, stride=16), :]
        scale = step[:, at]
        left = jnp.where(scale > 0.0, base[:, at] - added, 0.0)
        residual[:, at] = left
        fresh[:, at] = field[:, at] + scale * left


def finish(one, two, rows_of, lanes_of, base, field, step, fresh, residual):
    vmem = pl.BlockSpec(memory_space=pltpu.VMEM)
    there = pl.BlockSpec(memory_space=pl.ANY)
    first = pl.BlockSpec(base.shape, lambda t: (0, 0))
    return pl.pallas_call(
        finish_kernel,
        grid=(1,),
        out_shape=[jax.ShapeDtypeStruct(fresh.shape, F32)] * 2,
        in_specs=[vmem] * 7 + [there] * 2,
        out_specs=[first] * 2,
        scratch_shapes=[pltpu.VMEM((HEAD * 16, 128), F32)],
        input_output_aliases={7: 0, 8: 1},
        compiler_params=pltpu.CompilerParams(vmem_limit_bytes=24 * MIB),
        cost_estimate=pl.CostEstimate(flops=10**9, bytes_accessed=10**6, transcendentals=0),
        name="finish",
    )(one, two, rows_of, lanes_of, base, field, step, fresh, residual)


def per_device(
    iterate,
    rhs,
    material,
    orders,
    new_owner,
    face_send,
    face_recv,
    face_flip,
    stiff_off,
    stiff_diag,
    mass_diag,
):
    count = iterate.shape[1]
    owners = lax.axis_size("grp") * lax.axis_size("dev")
    packed, extra, near_w, far_w, body_w, rows_of, lanes_of = pack(
        (
            new_owner.reshape(1, count),
            orders.reshape(1, count),
            face_recv,
            face_flip,
            material,
            stiff_diag,
            mass_diag,
            iterate,
            rhs,
            stiff_off,
        ),
        owners,
    )

    def exchanged(rows):
        return lax.all_to_all(rows, ("grp", "dev"), split_axis=0, concat_axis=0, tiled=True)

    recv = exchanged(packed)
    flag, same = flag_of(recv)
    _, extra = lax.while_loop(
        lambda c: c[0] > 0.5,
        lambda c: (jnp.zeros((), F32), exchanged(c[1])),
        (flag[0, 0], extra),
    )
    base, field, step, one, two = head_rows(recv, same, extra, near_w, far_w, face_send, 16)
    one, two = swapped(one, "dev", 0), swapped(two, "dev", 1)
    fresh, residual = body_rows(recv, same, extra, body_w, 32)
    return tuple(finish(one, two, rows_of, lanes_of, base, field, step, fresh, residual))


def solution(mesh):
    both = ("grp", "dev")
    return jax.shard_map(
        per_device,
        mesh=mesh,
        in_specs=(
            P(None, both),
            P(None, both),
            P(None, both),
            P(both),
            P(both, None),
            P(None, both),
            P(None, both),
            P(None, both),
            P(),
            P(),
            P(),
        ),
        out_specs=(P(None, both), P(None, both)),
        check_vma=False,
    )
```

```python
import functools

import jax
import jax.numpy as jnp
from jax import lax
from jax.experimental import pallas as pl
from jax.experimental.pallas import tpu as pltpu
from jax.sharding import PartitionSpec as P

F32 = jnp.float32
BF16 = jnp.bfloat16
CHEBY = 2.0 / (2.0 + 0.2)
DOFS = 216
LIVE = (20, 45, 84, 140, 216)
PADDED = (24, 48, 88, 144, 216)
HEAD = 24
BODY = DOFS - HEAD
CAP = 16
COEFS = 16
NEAR = 88
NEAR_ROWS = CAP + CAP // 2
POOL = 24
POOL_MAX = 2 * CAP
POOL_STRIDE = POOL_MAX + 8
NEAR_W = (len(LIVE) + 3) * HEAD + COEFS
BODY_OFF = sum(n - HEAD for n in PADDED[1:])
NT = (((1,), (1,)), ((), ()))
MIB = 1 << 20


def swapped(array, axis, first):
    devices = lax.axis_size(axis)
    lower = range(first, devices - 1, 2)
    return lax.ppermute(array, axis, [p for i in lower for p in ((i, i + 1), (i + 1, i))])


def two_pieces(x):
    hi = x.astype(BF16)
    return hi, (x - hi.astype(F32)).astype(BF16)


def dot(a, b, dims=(((1,), (0,)), ((), ()))):
    return lax.dot_general(a, b, dims, preferred_element_type=F32)


def coefficients(material, order, first_row, overflow):
    c0, c1 = material[0:1], material[1:2]
    live = jnp.zeros(order.shape, jnp.int32)
    for k, n in enumerate(LIVE):
        live = jnp.where(order == k, n, live)
    rows = [c0, c1, live.astype(F32), first_row]
    for c in (c0, c1):
        rows += [jnp.where(order == k, c, 0.0) for k in range(len(LIVE))]
    rows += [jnp.zeros(order.shape, F32), jnp.broadcast_to(overflow, order.shape)]
    return jnp.concatenate(rows, axis=0)


def ranks_of(own_row, sizes, owners):
    chunk = 128
    upper = (
        lax.broadcasted_iota(jnp.int32, (chunk, chunk), 0)
        < lax.broadcasted_iota(jnp.int32, (chunk, chunk), 1)
    )
    sums = jnp.concatenate([upper.astype(F32), jnp.ones((chunk, chunk), F32)], axis=1).astype(BF16)
    carry = jnp.zeros((2 * owners, chunk), F32)
    ranks, firsts = [], []
    for c in range(own_row.shape[1] // chunk):
        here = slice(c * chunk, (c + 1) * chunk)
        named = (
            lax.broadcasted_iota(jnp.int32, (owners, chunk), 0) == own_row[:, here]
        ).astype(F32)
        marks = jnp.concatenate([named, named * sizes[:, here]], axis=0).astype(BF16)
        both = dot(marks, sums)
        earlier = both[:, :chunk] + carry
        carry = carry + both[:, chunk:]
        ranks.append(jnp.sum(named * earlier[:owners], axis=0, keepdims=True))
        firsts.append(jnp.sum(named * earlier[owners:], axis=0, keepdims=True))
    return (jnp.concatenate(v, axis=1) for v in (ranks, firsts)), jnp.max(carry[owners:])


def weights_of(off, divisor):
    lanes = lax.broadcasted_iota(jnp.int32, (HEAD, 128), 1)

    def units(rows, start):
        place = lax.broadcasted_iota(jnp.int32, (rows, 128), 0) + start
        return (place == lax.broadcasted_iota(jnp.int32, (rows, 128), 1)).astype(F32)

    near = [
        jnp.where(lanes < min(n, NEAR), off[k, 0:HEAD, 0:128], 0.0) for k, n in enumerate(LIVE)
    ]
    near += [pltpu.roll(divisor, COEFS, 1)[:HEAD]]
    near += [units(HEAD, 0), units(HEAD, NEAR), units(COEFS, 128 - COEFS)]
    pool = [
        jnp.where(lanes < LIVE[k] - NEAR, off[k, 0:HEAD, NEAR:DOFS], 0.0) for k in (4, 3)
    ]
    pad = jnp.zeros((DOFS, 256 - DOFS), F32)
    body = [
        jnp.concatenate([off[k], pad], axis=1)[HEAD:n] for k, n in enumerate(PADDED) if k > 0
    ]
    at = 128 - 2 * COEFS
    sums = divisor[HEAD:, at : at + COEFS]
    return (jnp.concatenate(v, axis=0) for v in (near, pool, body, [sums]))


def three_passes(w):
    hi, lo = two_pieces(w)
    return jnp.concatenate([hi, lo, hi], axis=1)


def side_by_side(pair, swap):
    both = pair[...]
    there, back = (jnp.concatenate([both[i : i + 1], both[1 - i : 2 - i]], axis=1) for i in (0, 1))
    return jnp.where(swap, back, there)


def odd_device():
    return lax.rem(lax.axis_index("dev"), 2) == 1


def pack_kernel(
    owner_in, orders_in, at_in, flip_in, material_in, diag_in, mass_in, field_in, source_in, off_in,
    out, extra, near_out, far_out, body_out, sums_out, rows_out, lanes_out,
    owner, orders, at, flip, material, diag, mass, field, source, off,
    near_w, far_w, body_w, sums_w, rows_of, lanes_of,
    t0, t1, t2, t3, whole, halves, merged, pool, table,
    slot_index, pool_index, slot_at, pool_at, in_sems, out_sems, index_sems,
):
    count = field.shape[1]
    owners = out.shape[0]
    chunk = 128
    loads = []
    for src, dst in (
        (owner_in, owner),
        (orders_in, orders),
        (at_in, at),
        (flip_in, flip),
        (material_in, material),
        (diag_in, diag),
        (mass_in, mass),
        (field_in, field),
        (source_in, source),
        (off_in, off),
    ):
        loads.append(pltpu.make_async_copy(src, dst, in_sems.at[len(loads)]))
        loads[-1].start()
    sends = []

    def send(src, dst):
        sends.append(pltpu.make_async_copy(src, dst, out_sems.at[len(sends)]))
        sends[-1].start()

    table[...] = jnp.zeros(table.shape, F32)
    pool[...] = jnp.zeros(pool.shape, F32)
    for c in loads[0:2]:
        c.wait()
    own_row, order = owner[...], orders[...]
    sizes = jnp.where(order == 4, 2.0, jnp.where(order == 3, 1.0, 0.0))
    (rank, first_row), largest = ranks_of(own_row, sizes, owners)
    slot_index[...] = own_row * CAP + rank.astype(jnp.int32)
    pool_index[...] = own_row * POOL_STRIDE + first_row.astype(jnp.int32)
    copies = [
        pltpu.make_async_copy(src, dst, index_sems.at[i])
        for i, (src, dst) in enumerate(((pool_index, pool_at), (slot_index, slot_at)))
    ]
    for c in copies:
        c.start()
    overflow = jnp.where(largest > POOL, 1.0, 0.0)
    last = lax.broadcasted_iota(jnp.int32, whole.shape, 1) == 127
    whole[...] = jnp.where(last, overflow, 0.0)

    for c in loads[2:7]:
        c.wait()
    swap = jnp.logical_not(odd_device())
    row = side_by_side(at, swap)
    signs = (1 - 2 * side_by_side(flip, swap)).astype(F32)
    faces = row.shape[1]
    mine = lax.broadcasted_iota(jnp.int32, (HEAD * 16, faces), 0) == row // 128
    rows_of[...] = mine.astype(F32).astype(BF16)
    spot = lax.broadcasted_iota(jnp.int32, (128, faces), 0) == lax.rem(row, 128)
    lanes_of[...] = jnp.where(spot, signs, 0.0)
    first = 128 - 2 * COEFS + 4
    orders_held = len(LIVE)
    table[first : first + orders_held, 0:DOFS] = diag[...]
    table[first + orders_held : first + 2 * orders_held, 0:DOFS] = mass[...]
    coefs = coefficients(material[...], order, first_row, overflow)

    for c in loads[7:]:
        c.wait()
    for c in range(count // chunk):
        here = slice(c * chunk, (c + 1) * chunk)
        t0[here, :] = jnp.concatenate(
            [field[0:NEAR, here], source[0:HEAD, here], coefs[:, here]], axis=0
        ).T
        middle = source[HEAD:NEAR, here]
        t1[here, :] = jnp.concatenate([middle, middle], axis=0).T
        top = jnp.where(order[:, here] == 4, field[NEAR + 64 : DOFS, here], source[NEAR : NEAR + 64, here])
        t2[here, :] = jnp.concatenate([field[NEAR : NEAR + 64, here], top], axis=0).T
        t3[here, :] = source[NEAR:DOFS, here].T
    near, far, body, divisor = weights_of(off, table[...].T[:DOFS])
    near_w[...] = three_passes(near)
    far_w[...] = three_passes(far)
    body_w[...] = three_passes(body)
    sums_w[...] = three_passes(divisor)
    for c in copies:
        c.wait()
    for src, dst in (
        (near_w, near_out),
        (far_w, far_out),
        (body_w, body_out),
        (sums_w, sums_out),
        (rows_of, rows_out),
        (lanes_of, lanes_out),
    ):
        send(src, dst)

    def place(row_at, steps):
        def step(g, carry):
            for j in range(32):
                i = g * 32 + j
                row = row_at[0, i]
                for rows, block, ahead in steps:
                    block[pl.ds(row + ahead, 1), :] = rows[pl.ds(i, 1), :]
            return carry

        lax.fori_loop(0, count // 32, step, 0)

    place(pool_at, [(t2, pool, 0), (t3, pool, 1)])
    pools = pool.reshape(owners, POOL_STRIDE, 128)
    send(pools.at[:, 0:POOL, :], out.at[:, NEAR_ROWS : NEAR_ROWS + POOL, :])
    send(pools.at[:, POOL:POOL_MAX, :], extra)
    place(slot_at, [(t0, whole, 0), (t1, halves, 0)])
    send(whole.reshape(owners, CAP, 128), out.at[:, 0:CAP, :])
    both = halves[...].reshape(owners, CAP, 128)
    low = lax.broadcasted_iota(jnp.int32, (owners, CAP // 2, 128), 2) < 64
    both = jnp.where(low, both[:, 0 : CAP // 2], both[:, CAP // 2 :])
    merged[...] = both.reshape(merged.shape)
    send(merged.reshape(owners, CAP // 2, 128), out.at[:, CAP:NEAR_ROWS, :])
    for c in sends:
        c.wait()


def pack(operands, owners):
    count = operands[0].shape[1]
    faces = 2 * operands[2].shape[1]
    hbm = pl.BlockSpec(memory_space=pltpu.HBM)
    made = [
        jax.ShapeDtypeStruct((NEAR_W, 384), BF16),
        jax.ShapeDtypeStruct((2 * HEAD, 384), BF16),
        jax.ShapeDtypeStruct((BODY_OFF, 768), BF16),
        jax.ShapeDtypeStruct((BODY, 3 * COEFS), BF16),
        jax.ShapeDtypeStruct((HEAD * 16, faces), BF16),
        jax.ShapeDtypeStruct((128, faces), F32),
    ]
    return pl.pallas_call(
        pack_kernel,
        out_shape=[
            jax.ShapeDtypeStruct((owners, NEAR_ROWS + POOL, 128), F32),
            jax.ShapeDtypeStruct((owners, POOL_MAX - POOL, 128), F32),
        ]
        + made,
        in_specs=[hbm] * len(operands),
        out_specs=[hbm] * 8,
        scratch_shapes=[pltpu.VMEM(a.shape, a.dtype) for a in list(operands) + made]
        + [pltpu.VMEM((count, 128), F32)] * 4
        + [pltpu.VMEM((owners * CAP, 128), F32)] * 2
        + [
            pltpu.VMEM((owners * CAP // 2, 128), F32),
            pltpu.VMEM((owners * POOL_STRIDE, 128), F32),
            pltpu.VMEM((128, 256), F32),
            pltpu.VMEM((1, count), jnp.int32),
            pltpu.VMEM((1, count), jnp.int32),
            pltpu.SMEM((1, count), jnp.int32),
            pltpu.SMEM((1, count), jnp.int32),
            pltpu.SemaphoreType.DMA((len(operands),)),
            pltpu.SemaphoreType.DMA((10,)),
            pltpu.SemaphoreType.DMA((2,)),
        ],
        compiler_params=pltpu.CompilerParams(vmem_limit_bytes=60 * MIB),
        name="pack",
    )(*operands)


def pool_columns(pools, first_row):
    rows, wide = pools.shape
    partners = first_row.shape[1] // CAP
    held = wide // partners
    lane = lax.broadcasted_iota(jnp.int32, (1, 128), 1)
    tiles = []
    for j in range(partners // 8):
        start = j * 8 * held
        tile = start // 128
        at = start % 128 + lane // CAP * held + first_row[:, j * 128 : (j + 1) * 128]
        second = jnp.broadcast_to(at >= 128, (8, 128))
        at = jnp.broadcast_to(jnp.bitwise_and(at, 127), (8, 128))

        def taken(r, tile):
            part = pools[r : r + 8, tile * 128 : (tile + 1) * 128]
            return jnp.take_along_axis(part, at, axis=1, mode="promise_in_bounds")

        tiles.append(
            jnp.concatenate(
                [jnp.where(second, taken(r, tile + 1), taken(r, tile)) for r in range(0, rows, 8)],
                axis=0,
            )
        )
    return jnp.concatenate(tiles, axis=1)


def stacked_pieces(values):
    hi, lo = two_pieces(values)
    return jnp.concatenate([hi, hi, lo], axis=0)


def flag_kernel(recv, flag, same):
    flags = jnp.max(jnp.max(recv[:, 0:8, :], axis=0), axis=0, keepdims=True)
    last = lax.broadcasted_iota(jnp.int32, flags.shape, 1) == 127
    flag[...] = jnp.max(jnp.where(last, flags, 0.0), axis=1, keepdims=True)
    same[...] = flag[...]


def flag_of(recv):
    vmem = pl.BlockSpec(memory_space=pltpu.VMEM)
    return pl.pallas_call(
        flag_kernel,
        out_shape=[jax.ShapeDtypeStruct((1, 1), F32)] * 2,
        in_specs=[vmem],
        out_specs=[vmem] * 2,
        compiler_params=pltpu.CompilerParams(vmem_limit_bytes=16 * MIB),
        name="flag_of",
    )(recv)


def load_overflow(flag, extra, more, sem):
    @pl.when(jnp.max(flag[...]) > 0.5)
    def _():
        copy = pltpu.make_async_copy(extra, more, sem)
        copy.start()
        copy.wait()


def row_pieces(rows):
    hi, lo = two_pieces(rows)
    return jnp.concatenate([hi, hi, lo], axis=1)


def head_kernel(
    recv, flag, extra, near_w, far_w, send,
    base, field, step, one, two, applied_at, more, sem, *, group,
):
    load_overflow(flag, extra, more, sem)
    slots = group * CAP
    for t in range(recv.shape[0] // group):
        at = slice(t * group, (t + 1) * group)
        here = slice(t * slots, (t + 1) * slots)
        near = recv[at, 0:CAP, :].reshape(-1, 128)
        pools = jnp.concatenate([recv[at, NEAR_ROWS:, :], more[at]], axis=1).reshape(-1, 128)
        y = dot(near_w[...], row_pieces(near), NT)
        z = dot(far_w[...], row_pieces(pools), NT)
        diag, x, rhs = (y[(5 + i) * HEAD : (6 + i) * HEAD] for i in range(3))
        coefs = y[8 * HEAD :]
        c0, live = coefs[0:1], coefs[2:3]
        far = pool_columns(z, (coefs[3:4] + 0.5).astype(jnp.int32))
        product = y[0:HEAD]
        for k in range(1, len(LIVE)):
            mine = y[k * HEAD : (k + 1) * HEAD]
            if k >= 3:
                mine = mine + far[(4 - k) * HEAD : (5 - k) * HEAD]
            product = jnp.where(coefs[4 + k : 5 + k] > 0.0, mine, product)
        rows = lax.broadcasted_iota(jnp.int32, (HEAD, slots), 0).astype(F32)
        alive = rows + 0.5 < live
        divisor = jnp.where(alive, diag, 1.0)
        applied = jnp.where(alive, c0 * product + divisor * x, 0.0)
        applied_at[:, here] = applied
        base[:, here] = jnp.where(alive, rhs - applied, 0.0)
        field[:, here] = jnp.where(alive, x, 0.0)
        step[:, here] = jnp.where(alive, CHEBY / divisor, 0.0)

    row = side_by_side(send, odd_device())
    slot = lax.rem(row, 2048)
    lane, block, dof = lax.rem(slot, 128), slot // 128, row // 2048
    rows = lax.broadcasted_iota(jnp.int32, (8, 128), 0)
    for i in range(row.shape[1] // 128):
        part = slice(i * 128, (i + 1) * 128)
        lanes = jnp.broadcast_to(lane[:, part], (8, 128))
        blocks = jnp.broadcast_to(block[:, part], (8, 128))
        dofs = jnp.broadcast_to(dof[:, part], (8, 128))
        total = jnp.zeros((8, 128), F32)
        for d in range(HEAD // 8):
            found = jnp.zeros((8, 128), F32)
            for b in range(applied_at.shape[1] // 128):
                held = applied_at[d * 8 : (d + 1) * 8, b * 128 : (b + 1) * 128]
                taken = jnp.take_along_axis(held, lanes, axis=1, mode="promise_in_bounds")
                found = jnp.where(blocks == b, taken, found)
            total = total + jnp.where(rows + d * 8 == dofs, found, 0.0)
        values = jnp.sum(total, axis=0, keepdims=True)
        if i < 4:
            one[i : i + 1, :] = values
        else:
            two[i - 4 : i - 3, :] = values


def head_rows(recv, flag, extra, near_w, far_w, face_send, group):
    slots = recv.shape[0] * CAP
    vmem = pl.BlockSpec(memory_space=pltpu.VMEM)
    there = pl.BlockSpec(memory_space=pltpu.HBM)
    return pl.pallas_call(
        functools.partial(head_kernel, group=group),
        out_shape=[jax.ShapeDtypeStruct((HEAD, slots), F32)] * 3
        + [jax.ShapeDtypeStruct((4, 128), F32)] * 2,
        in_specs=[vmem] * 2 + [there] + [vmem] * 3,
        out_specs=[vmem] * 5,
        scratch_shapes=[
            pltpu.VMEM((HEAD, slots), F32),
            pltpu.VMEM(extra.shape, F32),
            pltpu.SemaphoreType.DMA,
        ],
        compiler_params=pltpu.CompilerParams(vmem_limit_bytes=24 * MIB),
        cost_estimate=pl.CostEstimate(flops=2 * 10**9, bytes_accessed=4 * 10**6, transcendentals=0),
        name="head_rows",
    )(recv, flag, extra, near_w, far_w, face_send)


def chosen_columns(pools, first_row):
    held = pools.shape[1] * CAP // first_row.shape[1]
    lane = lax.broadcasted_iota(jnp.int32, (1, 128), 1)
    row = lax.broadcasted_iota(jnp.int32, (8 * held, 256), 0)
    fars = []
    for j in range(first_row.shape[1] // 128):
        at = lane // CAP * held + first_row[:, j * 128 : (j + 1) * 128]
        chosen = (row == jnp.concatenate([at, at + 1], axis=1)).astype(F32).astype(BF16)
        hi, lo = two_pieces(pools[:, j * 8 * held : (j + 1) * 8 * held])
        both = dot(jnp.concatenate([hi, lo], axis=0), chosen)
        fars.append(both[0:128] + both[128:256])
    return (
        jnp.concatenate([f[:, i * 128 : (i + 1) * 128] for f in fars], axis=1) for i in range(2)
    )


def unpacked(recv, more, at):
    near = recv[at, 0:CAP, :].reshape(-1, 128).T
    middle = recv[at, CAP:NEAR_ROWS, :]
    turned = pltpu.roll(middle.reshape(-1, 128), 64, 1).reshape(middle.shape)
    middle = jnp.stack([middle, turned], axis=1).reshape(-1, 128).T[0:64]
    pools = jnp.concatenate([recv[at, NEAR_ROWS:, :], more[at]], axis=1).reshape(-1, 128).T
    coefs = near[128 - COEFS :]
    far, far_rhs = chosen_columns(pools, coefs[3:4].astype(jnp.int32))
    slots = near.shape[1]
    rows = lax.broadcasted_iota(jnp.int32, (DOFS, slots), 0).astype(F32)
    alive = rows + 0.5 < coefs[2:3]
    values = jnp.where(alive, jnp.concatenate([near[0:NEAR], far], axis=0), 0.0)
    top = jnp.where(coefs[8:9] > 0.0, far_rhs[0:64], far[64:128])
    rhs = jnp.concatenate([middle, top, far_rhs[64:]], axis=0)
    full = jnp.concatenate([values, jnp.zeros((256 - DOFS, slots), F32)], axis=0)
    return stacked_pieces(full), stacked_pieces(coefs), coefs, values[HEAD:], rhs


def body_step(off_w, sums_w, x, c, coefs, field, rhs):
    y = dot(off_w[...], x)
    c0, live = coefs[0:1], coefs[2:3]
    product = None
    start = BODY_OFF
    for k in range(len(LIVE) - 1, 0, -1):
        size = PADDED[k] - HEAD
        start -= size
        mine = y[start : start + size]
        if product is None:
            product = mine
        else:
            best = jnp.where(coefs[4 + k : 5 + k] > 0.0, mine, product[0:size])
            product = jnp.concatenate([best, product[size:]], axis=0)
    rows = lax.broadcasted_iota(jnp.int32, field.shape, 0).astype(F32) + HEAD
    alive = rows + 0.5 < live
    divisor = jnp.where(alive, dot(sums_w[...], c), 1.0)
    left = jnp.where(alive, rhs - c0 * product - divisor * field, 0.0)
    return field + CHEBY * left / divisor, left


def body_kernel(recv, flag, extra, off_w, sums_w, fresh, residual, more, new, rest, sem, sems, *, group):
    more[...] = jnp.zeros(more.shape, F32)
    load_overflow(flag, extra, more, sem)
    slots = group * CAP
    steps = recv.shape[0] // group
    sends = []
    ready = unpacked(recv, more, slice(0, group))
    for t in range(steps):
        now = ready
        if t + 1 < steps:
            ready = unpacked(recv, more, slice((t + 1) * group, (t + 2) * group))
        here = slice(t * slots, (t + 1) * slots)
        new[:, here], rest[:, here] = body_step(off_w, sums_w, *now)
        for src, dst in ((new, fresh), (rest, residual)):
            sends.append(
                pltpu.make_async_copy(
                    src.at[:, here], dst.at[HEAD:DOFS, here], sems.at[len(sends)]
                )
            )
            sends[-1].start()
    for c in sends:
        c.wait()


def body_rows(recv, flag, extra, off_w, sums_w, group):
    partners = recv.shape[0]
    slots = partners * CAP
    vmem = pl.BlockSpec(memory_space=pltpu.VMEM)
    hbm = pl.BlockSpec(memory_space=pltpu.HBM)
    return pl.pallas_call(
        functools.partial(body_kernel, group=group),
        out_shape=[jax.ShapeDtypeStruct((DOFS, slots), F32)] * 2,
        in_specs=[vmem, vmem, hbm, vmem, vmem],
        out_specs=[hbm] * 2,
        scratch_shapes=[
            pltpu.VMEM(extra.shape, F32),
            pltpu.VMEM((BODY, slots), F32),
            pltpu.VMEM((BODY, slots), F32),
            pltpu.SemaphoreType.DMA,
            pltpu.SemaphoreType.DMA((2 * partners // group,)),
        ],
        compiler_params=pltpu.CompilerParams(vmem_limit_bytes=24 * MIB),
        cost_estimate=pl.CostEstimate(flops=4 * 10**9, bytes_accessed=8 * 10**6, transcendentals=0),
        name="body_rows",
    )(recv, flag, extra, off_w, sums_w)


def finish_kernel(one, two, rows_of, lanes_of, base, field, step, _, __, fresh, residual, flat):
    values = jnp.concatenate(
        [one[i : i + 1, :] for i in range(4)] + [two[i : i + 1, :] for i in range(4)], axis=1
    )
    hi, mid = (p.astype(F32) for p in two_pieces(values))
    spread = lanes_of[...]
    pieces = jnp.concatenate([spread * hi, spread * mid, spread * (values - hi - mid)], axis=0)
    found = dot(rows_of[...], pieces.astype(BF16), NT)
    flat[...] = found[:, 0:128] + found[:, 128:256] + found[:, 256:384]
    for b in range(16):
        at = slice(b * 128, (b + 1) * 128)
        added = flat[pl.ds(b, HEAD, stride=16), :]
        scale = step[:, at]
        left = jnp.where(scale > 0.0, base[:, at] - added, 0.0)
        residual[:, at] = left
        fresh[:, at] = field[:, at] + scale * left


def finish(one, two, rows_of, lanes_of, base, field, step, fresh, residual):
    vmem = pl.BlockSpec(memory_space=pltpu.VMEM)
    there = pl.BlockSpec(memory_space=pl.ANY)
    first = pl.BlockSpec(base.shape, lambda t: (0, 0))
    return pl.pallas_call(
        finish_kernel,
        grid=(1,),
        out_shape=[jax.ShapeDtypeStruct(fresh.shape, F32)] * 2,
        in_specs=[vmem] * 7 + [there] * 2,
        out_specs=[first] * 2,
        scratch_shapes=[pltpu.VMEM((HEAD * 16, 128), F32)],
        input_output_aliases={7: 0, 8: 1},
        compiler_params=pltpu.CompilerParams(vmem_limit_bytes=24 * MIB),
        cost_estimate=pl.CostEstimate(flops=10**9, bytes_accessed=10**6, transcendentals=0),
        name="finish",
    )(one, two, rows_of, lanes_of, base, field, step, fresh, residual)


def per_device(
    iterate,
    rhs,
    material,
    orders,
    new_owner,
    face_send,
    face_recv,
    face_flip,
    stiff_off,
    stiff_diag,
    mass_diag,
):
    count = iterate.shape[1]
    owners = lax.axis_size("grp") * lax.axis_size("dev")
    packed, extra, near_w, far_w, off_w, sums_w, rows_of, lanes_of = pack(
        (
            new_owner.reshape(1, count),
            orders.reshape(1, count),
            face_recv,
            face_flip,
            material,
            stiff_diag,
            mass_diag,
            iterate,
            rhs,
            stiff_off,
        ),
        owners,
    )

    def exchanged(rows):
        return lax.all_to_all(rows, ("grp", "dev"), split_axis=0, concat_axis=0, tiled=True)

    recv = exchanged(packed)
    flag, same = flag_of(recv)
    _, extra = lax.while_loop(
        lambda c: c[0] > 0.5,
        lambda c: (jnp.zeros((), F32), exchanged(c[1])),
        (flag[0, 0], extra),
    )
    base, field, step, one, two = head_rows(recv, same, extra, near_w, far_w, face_send, 16)
    one, two = swapped(one, "dev", 0), swapped(two, "dev", 1)
    fresh, residual = body_rows(recv, same, extra, off_w, sums_w, 32)
    return tuple(finish(one, two, rows_of, lanes_of, base, field, step, fresh, residual))


def solution(mesh):
    both = ("grp", "dev")
    return jax.shard_map(
        per_device,
        mesh=mesh,
        in_specs=(
            P(None, both),
            P(None, both),
            P(None, both),
            P(both),
            P(both, None),
            P(None, both),
            P(None, both),
            P(None, both),
            P(),
            P(),
            P(),
        ),
        out_specs=(P(None, both), P(None, both)),
        check_vma=False,
    )
```

```python
import functools

import jax
import jax.numpy as jnp
from jax import lax
from jax.experimental import pallas as pl
from jax.experimental.pallas import tpu as pltpu
from jax.sharding import PartitionSpec as P

F32 = jnp.float32
BF16 = jnp.bfloat16
CHEBY = 2.0 / (2.0 + 0.2)
DOFS = 216
LIVE = (20, 45, 84, 140, 216)
PADDED = (24, 48, 88, 144, 216)
HEAD = 24
BODY = DOFS - HEAD
CAP = 16
COEFS = 16
NEAR = 88
NEAR_ROWS = CAP + CAP // 2
POOL = 24
POOL_MAX = 2 * CAP
POOL_STRIDE = POOL_MAX + 8
NEAR_W = (len(LIVE) + 3) * HEAD + COEFS
BODY_OFF = sum(n - HEAD for n in PADDED[1:])
NT = (((1,), (1,)), ((), ()))
MIB = 1 << 20


def swapped(array, axis, first):
    devices = lax.axis_size(axis)
    lower = range(first, devices - 1, 2)
    return lax.ppermute(array, axis, [p for i in lower for p in ((i, i + 1), (i + 1, i))])


def two_pieces(x):
    hi = x.astype(BF16)
    return hi, (x - hi.astype(F32)).astype(BF16)


def dot(a, b, dims=(((1,), (0,)), ((), ()))):
    return lax.dot_general(a, b, dims, preferred_element_type=F32)


def coefficients(material, order, first_row, overflow):
    c0, c1 = material[0:1], material[1:2]
    live = jnp.zeros(order.shape, jnp.int32)
    for k, n in enumerate(LIVE):
        live = jnp.where(order == k, n, live)
    rows = [c0, c1, live.astype(F32), first_row]
    for c in (c0, c1):
        rows += [jnp.where(order == k, c, 0.0) for k in range(len(LIVE))]
    rows += [jnp.zeros(order.shape, F32), jnp.broadcast_to(overflow, order.shape)]
    return jnp.concatenate(rows, axis=0)


def ranks_of(own_row, sizes, owners):
    chunk = 128
    upper = (
        lax.broadcasted_iota(jnp.int32, (chunk, chunk), 0)
        < lax.broadcasted_iota(jnp.int32, (chunk, chunk), 1)
    )
    sums = jnp.concatenate([upper.astype(F32), jnp.ones((chunk, chunk), F32)], axis=1).astype(BF16)
    carry = jnp.zeros((2 * owners, chunk), F32)
    ranks, firsts = [], []
    for c in range(own_row.shape[1] // chunk):
        here = slice(c * chunk, (c + 1) * chunk)
        named = (
            lax.broadcasted_iota(jnp.int32, (owners, chunk), 0) == own_row[:, here]
        ).astype(F32)
        marks = jnp.concatenate([named, named * sizes[:, here]], axis=0).astype(BF16)
        both = dot(marks, sums)
        earlier = both[:, :chunk] + carry
        carry = carry + both[:, chunk:]
        ranks.append(jnp.sum(named * earlier[:owners], axis=0, keepdims=True))
        firsts.append(jnp.sum(named * earlier[owners:], axis=0, keepdims=True))
    return (jnp.concatenate(v, axis=1) for v in (ranks, firsts)), jnp.max(carry[owners:])


def weights_of(off, divisor):
    lanes = lax.broadcasted_iota(jnp.int32, (HEAD, 128), 1)

    def units(rows, start):
        place = lax.broadcasted_iota(jnp.int32, (rows, 128), 0) + start
        return (place == lax.broadcasted_iota(jnp.int32, (rows, 128), 1)).astype(F32)

    near = [
        jnp.where(lanes < min(n, NEAR), off[k, 0:HEAD, 0:128], 0.0) for k, n in enumerate(LIVE)
    ]
    near += [pltpu.roll(divisor, COEFS, 1)[:HEAD]]
    near += [units(HEAD, 0), units(HEAD, NEAR), units(COEFS, 128 - COEFS)]
    pool = [
        jnp.where(lanes < LIVE[k] - NEAR, off[k, 0:HEAD, NEAR:DOFS], 0.0) for k in (4, 3)
    ]
    body = []
    for k, n in enumerate(PADDED[1:], 1):
        wide = 128 if n < 128 else DOFS
        pad = jnp.zeros((n - HEAD, 256 - wide), F32)
        body.append(jnp.concatenate([off[k, HEAD:n, 0:wide], pad], axis=1))
    at = 128 - 2 * COEFS
    sums = divisor[HEAD:, at : at + COEFS]
    return (jnp.concatenate(v, axis=0) for v in (near, pool, body, [sums]))


def three_passes(w):
    hi, lo = two_pieces(w)
    return jnp.concatenate([hi, lo, hi], axis=1)


def side_by_side(pair, swap):
    both = pair[...]
    there, back = (jnp.concatenate([both[i : i + 1], both[1 - i : 2 - i]], axis=1) for i in (0, 1))
    return jnp.where(swap, back, there)


def odd_device():
    return lax.rem(lax.axis_index("dev"), 2) == 1


def pack_kernel(
    owner_in, orders_in, at_in, flip_in, material_in, diag_in, mass_in, field_in, source_in, off_in,
    out, extra, near_out, far_out, body_out, sums_out, rows_out, lanes_out,
    owner, orders, at, flip, material, diag, mass, field, source, off,
    near_w, far_w, body_w, sums_w, rows_of, lanes_of,
    t0, t1, t2, t3, whole, halves, merged, pool, table,
    coefs_at, slot_index, pool_index, slot_at, pool_at, in_sems, out_sems, index_sems, spill_sem,
):
    count = field.shape[1]
    owners = out.shape[0]
    chunk = 128
    loads = []
    pairs = [
        (owner_in, owner),
        (orders_in, orders),
        (at_in, at),
        (flip_in, flip),
        (material_in, material),
        (diag_in, diag),
        (mass_in, mass),
        (field_in, field),
        (source_in, source),
    ]
    for k, n in enumerate(PADDED):
        part = slice(0, n), slice(0, 128 if n < 128 else DOFS)
        pairs.append((off_in.at[k, part[0], part[1]], off.at[k, part[0], part[1]]))
    for src, dst in pairs:
        loads.append(pltpu.make_async_copy(src, dst, in_sems.at[len(loads)]))
        loads[-1].start()
    sends = []

    def send(src, dst):
        sends.append(pltpu.make_async_copy(src, dst, out_sems.at[len(sends)]))
        sends[-1].start()

    table[...] = jnp.zeros(table.shape, F32)
    pool[...] = jnp.zeros(pool.shape, F32)
    for c in loads[0:2]:
        c.wait()
    own_row, order = owner[...], orders[...]
    sizes = jnp.where(order == 4, 2.0, jnp.where(order == 3, 1.0, 0.0))
    (rank, first_row), largest = ranks_of(own_row, sizes, owners)
    slot_index[...] = own_row * CAP + rank.astype(jnp.int32)
    pool_index[...] = own_row * POOL_STRIDE + first_row.astype(jnp.int32)
    copies = [
        pltpu.make_async_copy(src, dst, index_sems.at[i])
        for i, (src, dst) in enumerate(((pool_index, pool_at), (slot_index, slot_at)))
    ]
    for c in copies:
        c.start()
    overflow = jnp.where(largest > POOL, 1.0, 0.0)
    last = lax.broadcasted_iota(jnp.int32, whole.shape, 1) == 127
    whole[...] = jnp.where(last, overflow, 0.0)

    for c in loads[2:7]:
        c.wait()
    swap = jnp.logical_not(odd_device())
    row = side_by_side(at, swap)
    signs = (1 - 2 * side_by_side(flip, swap)).astype(F32)
    faces = row.shape[1]
    mine = lax.broadcasted_iota(jnp.int32, (HEAD * 16, faces), 0) == row // 128
    rows_of[...] = mine.astype(F32).astype(BF16)
    spot = lax.broadcasted_iota(jnp.int32, (128, faces), 0) == lax.rem(row, 128)
    lanes_of[...] = jnp.where(spot, signs, 0.0).astype(BF16)
    first = 128 - 2 * COEFS + 4
    orders_held = len(LIVE)
    table[first : first + orders_held, 0:DOFS] = diag[...]
    table[first + orders_held : first + 2 * orders_held, 0:DOFS] = mass[...]
    coefs_at[...] = coefficients(material[...], order, first_row, overflow)

    for c in loads[7:]:
        c.wait()
    for c in range(count // chunk):
        here = slice(c * chunk, (c + 1) * chunk)
        top = jnp.where(order[:, here] == 4, field[NEAR + 64 : DOFS, here], source[NEAR : NEAR + 64, here])
        t2[here, :] = jnp.concatenate([field[NEAR : NEAR + 64, here], top], axis=0).T
        t3[here, :] = source[NEAR:DOFS, here].T
    near, far, body, divisor = weights_of(off, table[...].T[:DOFS])
    near_w[...] = three_passes(near)
    far_w[...] = three_passes(far)
    body_w[...] = three_passes(body)
    sums_w[...] = three_passes(divisor)
    for c in copies:
        c.wait()
    for src, dst in (
        (near_w, near_out),
        (far_w, far_out),
        (body_w, body_out),
        (sums_w, sums_out),
        (rows_of, rows_out),
        (lanes_of, lanes_out),
    ):
        send(src, dst)

    def place(row_at, steps, size, also=None):
        def step(g, carry):
            if also is not None:
                also(pl.ds(pl.multiple_of(g * size, size), size))
            for j in range(size):
                i = g * size + j
                row = row_at[0, i]
                for rows, block, ahead in steps:
                    block[pl.ds(row + ahead, 1), :] = rows[pl.ds(i, 1), :]
            return carry

        lax.fori_loop(0, count // size, step, 0)

    def turn(here):
        t0[here, :] = jnp.concatenate(
            [field[0:NEAR, here], source[0:HEAD, here], coefs_at[:, here]], axis=0
        ).T
        middle = source[HEAD:NEAR, here]
        t1[here, :] = jnp.concatenate([middle, middle], axis=0).T

    place(pool_at, [(t2, pool, 0), (t3, pool, 1)], chunk, turn)
    pools = pool.reshape(owners, POOL_STRIDE, 128)
    send(pools.at[:, 0:POOL, :], out.at[:, NEAR_ROWS : NEAR_ROWS + POOL, :])
    spill = pltpu.make_async_copy(pools.at[:, POOL:POOL_MAX, :], extra, spill_sem)

    @pl.when(overflow > 0.5)
    def _():
        spill.start()

    place(slot_at, [(t0, whole, 0), (t1, halves, 0)], 64)
    send(whole.reshape(owners, CAP, 128), out.at[:, 0:CAP, :])
    both = halves[...].reshape(owners, CAP, 128)
    low = lax.broadcasted_iota(jnp.int32, (owners, CAP // 2, 128), 2) < 64
    both = jnp.where(low, both[:, 0 : CAP // 2], both[:, CAP // 2 :])
    merged[...] = both.reshape(merged.shape)
    send(merged.reshape(owners, CAP // 2, 128), out.at[:, CAP:NEAR_ROWS, :])
    for c in sends:
        c.wait()

    @pl.when(overflow > 0.5)
    def _():
        spill.wait()


def pack(operands, owners):
    count = operands[0].shape[1]
    faces = 2 * operands[2].shape[1]
    hbm = pl.BlockSpec(memory_space=pltpu.HBM)
    made = [
        jax.ShapeDtypeStruct((NEAR_W, 384), BF16),
        jax.ShapeDtypeStruct((2 * HEAD, 384), BF16),
        jax.ShapeDtypeStruct((BODY_OFF, 768), BF16),
        jax.ShapeDtypeStruct((BODY, 3 * COEFS), BF16),
        jax.ShapeDtypeStruct((HEAD * 16, faces), BF16),
        jax.ShapeDtypeStruct((128, faces), BF16),
    ]
    return pl.pallas_call(
        pack_kernel,
        out_shape=[
            jax.ShapeDtypeStruct((owners, NEAR_ROWS + POOL, 128), F32),
            jax.ShapeDtypeStruct((owners, POOL_MAX - POOL, 128), F32),
        ]
        + made,
        in_specs=[hbm] * len(operands),
        out_specs=[hbm] * 8,
        scratch_shapes=[pltpu.VMEM(a.shape, a.dtype) for a in list(operands) + made]
        + [pltpu.VMEM((count, 128), F32)] * 4
        + [pltpu.VMEM((owners * CAP, 128), F32)] * 2
        + [
            pltpu.VMEM((owners * CAP // 2, 128), F32),
            pltpu.VMEM((owners * POOL_STRIDE, 128), F32),
            pltpu.VMEM((128, 256), F32),
            pltpu.VMEM((COEFS, count), F32),
            pltpu.VMEM((1, count), jnp.int32),
            pltpu.VMEM((1, count), jnp.int32),
            pltpu.SMEM((1, count), jnp.int32),
            pltpu.SMEM((1, count), jnp.int32),
            pltpu.SemaphoreType.DMA((len(operands) - 1 + len(LIVE),)),
            pltpu.SemaphoreType.DMA((9,)),
            pltpu.SemaphoreType.DMA((2,)),
            pltpu.SemaphoreType.DMA,
        ],
        compiler_params=pltpu.CompilerParams(vmem_limit_bytes=60 * MIB),
        name="pack",
    )(*operands)


def pool_columns(pools, first_row):
    rows, wide = pools.shape
    partners = first_row.shape[1] // CAP
    held = wide // partners
    lane = lax.broadcasted_iota(jnp.int32, (1, 128), 1)
    tiles = []
    for j in range(partners // 8):
        start = j * 8 * held
        tile = start // 128
        at = start % 128 + lane // CAP * held + first_row[:, j * 128 : (j + 1) * 128]
        second = jnp.broadcast_to(at >= 128, (8, 128))
        at = jnp.broadcast_to(jnp.bitwise_and(at, 127), (8, 128))

        def taken(r, tile):
            part = pools[r : r + 8, tile * 128 : (tile + 1) * 128]
            return jnp.take_along_axis(part, at, axis=1, mode="promise_in_bounds")

        tiles.append(
            jnp.concatenate(
                [jnp.where(second, taken(r, tile + 1), taken(r, tile)) for r in range(0, rows, 8)],
                axis=0,
            )
        )
    return jnp.concatenate(tiles, axis=1)


def stacked_pieces(values):
    hi, lo = two_pieces(values)
    return jnp.concatenate([hi, hi, lo], axis=0)


def flag_kernel(recv, flag, same):
    flags = jnp.max(jnp.max(recv[:, 0:8, :], axis=0), axis=0, keepdims=True)
    last = lax.broadcasted_iota(jnp.int32, flags.shape, 1) == 127
    flag[...] = jnp.max(jnp.where(last, flags, 0.0), axis=1, keepdims=True)
    same[...] = flag[...]


def flag_of(recv):
    vmem = pl.BlockSpec(memory_space=pltpu.VMEM)
    return pl.pallas_call(
        flag_kernel,
        out_shape=[jax.ShapeDtypeStruct((1, 1), F32)] * 2,
        in_specs=[vmem],
        out_specs=[vmem] * 2,
        compiler_params=pltpu.CompilerParams(vmem_limit_bytes=16 * MIB),
        name="flag_of",
    )(recv)


def load_overflow(flag, extra, more, sem):
    @pl.when(jnp.max(flag[...]) > 0.5)
    def _():
        copy = pltpu.make_async_copy(extra, more, sem)
        copy.start()
        copy.wait()


def row_pieces(rows):
    hi, lo = two_pieces(rows)
    return jnp.concatenate([hi, hi, lo], axis=1)


def head_kernel(
    recv, flag, extra, near_w, far_w, send,
    base, field, step, one, two, applied_at, more, sem, *, group,
):
    load_overflow(flag, extra, more, sem)
    slots = group * CAP
    for t in range(recv.shape[0] // group):
        at = slice(t * group, (t + 1) * group)
        here = slice(t * slots, (t + 1) * slots)
        near = recv[at, 0:CAP, :].reshape(-1, 128)
        pools = jnp.concatenate([recv[at, NEAR_ROWS:, :], more[at]], axis=1).reshape(-1, 128)
        y = dot(near_w[...], row_pieces(near), NT)
        z = dot(far_w[...], row_pieces(pools), NT)
        diag, x, rhs = (y[(5 + i) * HEAD : (6 + i) * HEAD] for i in range(3))
        coefs = y[8 * HEAD :]
        c0, live = coefs[0:1], coefs[2:3]
        far = pool_columns(z, (coefs[3:4] + 0.5).astype(jnp.int32))
        product = y[0:HEAD]
        for k in range(1, len(LIVE)):
            mine = y[k * HEAD : (k + 1) * HEAD]
            if k >= 3:
                mine = mine + far[(4 - k) * HEAD : (5 - k) * HEAD]
            product = jnp.where(coefs[4 + k : 5 + k] > 0.0, mine, product)
        rows = lax.broadcasted_iota(jnp.int32, (HEAD, slots), 0).astype(F32)
        alive = rows + 0.5 < live
        divisor = jnp.where(alive, diag, 1.0)
        applied = jnp.where(alive, c0 * product + divisor * x, 0.0)
        applied_at[:, here] = applied
        base[:, here] = jnp.where(alive, rhs - applied, 0.0)
        field[:, here] = jnp.where(alive, x, 0.0)
        step[:, here] = jnp.where(alive, CHEBY / divisor, 0.0)

    row = side_by_side(send, odd_device())
    slot = lax.rem(row, 2048)
    lane, block, dof = lax.rem(slot, 128), slot // 128, row // 2048
    rows = lax.broadcasted_iota(jnp.int32, (8, 128), 0)
    for i in range(row.shape[1] // 128):
        part = slice(i * 128, (i + 1) * 128)
        lanes = jnp.broadcast_to(lane[:, part], (8, 128))
        blocks = jnp.broadcast_to(block[:, part], (8, 128))
        dofs = jnp.broadcast_to(dof[:, part], (8, 128))
        total = jnp.zeros((8, 128), F32)
        for d in range(HEAD // 8):
            found = jnp.zeros((8, 128), F32)
            for b in range(applied_at.shape[1] // 128):
                held = applied_at[d * 8 : (d + 1) * 8, b * 128 : (b + 1) * 128]
                taken = jnp.take_along_axis(held, lanes, axis=1, mode="promise_in_bounds")
                found = jnp.where(blocks == b, taken, found)
            total = total + jnp.where(rows + d * 8 == dofs, found, 0.0)
        values = jnp.sum(total, axis=0, keepdims=True)
        if i < 4:
            one[i : i + 1, :] = values
        else:
            two[i - 4 : i - 3, :] = values


def head_rows(recv, flag, extra, near_w, far_w, face_send, group):
    slots = recv.shape[0] * CAP
    vmem = pl.BlockSpec(memory_space=pltpu.VMEM)
    there = pl.BlockSpec(memory_space=pltpu.HBM)
    return pl.pallas_call(
        functools.partial(head_kernel, group=group),
        out_shape=[jax.ShapeDtypeStruct((HEAD, slots), F32)] * 3
        + [jax.ShapeDtypeStruct((4, 128), F32)] * 2,
        in_specs=[vmem] * 2 + [there] + [vmem] * 3,
        out_specs=[vmem] * 5,
        scratch_shapes=[
            pltpu.VMEM((HEAD, slots), F32),
            pltpu.VMEM(extra.shape, F32),
            pltpu.SemaphoreType.DMA,
        ],
        compiler_params=pltpu.CompilerParams(vmem_limit_bytes=24 * MIB),
        cost_estimate=pl.CostEstimate(flops=2 * 10**9, bytes_accessed=4 * 10**6, transcendentals=0),
        name="head_rows",
    )(recv, flag, extra, near_w, far_w, face_send)


def chosen_columns(pools, first_row):
    held = pools.shape[1] * CAP // first_row.shape[1]
    lane = lax.broadcasted_iota(jnp.int32, (1, 128), 1)
    row = lax.broadcasted_iota(jnp.int32, (8 * held, 256), 0)
    fars = []
    for j in range(first_row.shape[1] // 128):
        at = lane // CAP * held + first_row[:, j * 128 : (j + 1) * 128]
        chosen = (row == jnp.concatenate([at, at + 1], axis=1)).astype(F32).astype(BF16)
        hi, lo = two_pieces(pools[:, j * 8 * held : (j + 1) * 8 * held])
        both = dot(jnp.concatenate([hi, lo], axis=0), chosen)
        fars.append(both[0:128] + both[128:256])
    return (
        jnp.concatenate([f[:, i * 128 : (i + 1) * 128] for f in fars], axis=1) for i in range(2)
    )


def unpacked(recv, more, at):
    near = recv[at, 0:CAP, :].reshape(-1, 128).T
    middle = recv[at, CAP:NEAR_ROWS, :]
    turned = pltpu.roll(middle.reshape(-1, 128), 64, 1).reshape(middle.shape)
    middle = jnp.stack([middle, turned], axis=1).reshape(-1, 128).T[0:64]
    pools = jnp.concatenate([recv[at, NEAR_ROWS:, :], more[at]], axis=1).reshape(-1, 128).T
    coefs = near[128 - COEFS :]
    far, far_rhs = chosen_columns(pools, coefs[3:4].astype(jnp.int32))
    slots = near.shape[1]
    rows = lax.broadcasted_iota(jnp.int32, (DOFS, slots), 0).astype(F32)
    alive = rows + 0.5 < coefs[2:3]
    values = jnp.where(alive, jnp.concatenate([near[0:NEAR], far], axis=0), 0.0)
    top = jnp.where(coefs[8:9] > 0.0, far_rhs[0:64], far[64:128])
    rhs = jnp.concatenate([middle, top, far_rhs[64:]], axis=0)
    full = jnp.concatenate([values, jnp.zeros((256 - DOFS, slots), F32)], axis=0)
    return stacked_pieces(full), stacked_pieces(coefs), coefs, values[HEAD:], rhs


def body_step(off_w, sums_w, x, c, coefs, field, rhs):
    y = dot(off_w[...], x)
    c0, live = coefs[0:1], coefs[2:3]
    product = None
    start = BODY_OFF
    for k in range(len(LIVE) - 1, 0, -1):
        size = PADDED[k] - HEAD
        start -= size
        mine = y[start : start + size]
        if product is None:
            product = mine
        else:
            best = jnp.where(coefs[4 + k : 5 + k] > 0.0, mine, product[0:size])
            product = jnp.concatenate([best, product[size:]], axis=0)
    rows = lax.broadcasted_iota(jnp.int32, field.shape, 0).astype(F32) + HEAD
    alive = rows + 0.5 < live
    divisor = jnp.where(alive, dot(sums_w[...], c), 1.0)
    left = jnp.where(alive, rhs - c0 * product - divisor * field, 0.0)
    return field + CHEBY * left / divisor, left


def body_kernel(recv, flag, extra, off_w, sums_w, fresh, residual, more, new, rest, sem, sems, *, group):
    more[...] = jnp.zeros(more.shape, F32)
    load_overflow(flag, extra, more, sem)
    slots = group * CAP
    steps = recv.shape[0] // group
    sends = []
    ready = unpacked(recv, more, slice(0, group))
    for t in range(steps):
        now = ready
        if t + 1 < steps:
            ready = unpacked(recv, more, slice((t + 1) * group, (t + 2) * group))
        here = slice(t * slots, (t + 1) * slots)
        new[:, here], rest[:, here] = body_step(off_w, sums_w, *now)
        for src, dst in ((new, fresh), (rest, residual)):
            sends.append(
                pltpu.make_async_copy(
                    src.at[:, here], dst.at[HEAD:DOFS, here], sems.at[len(sends)]
                )
            )
            sends[-1].start()
    for c in sends:
        c.wait()


def body_rows(recv, flag, extra, off_w, sums_w, group):
    partners = recv.shape[0]
    slots = partners * CAP
    vmem = pl.BlockSpec(memory_space=pltpu.VMEM)
    hbm = pl.BlockSpec(memory_space=pltpu.HBM)
    return pl.pallas_call(
        functools.partial(body_kernel, group=group),
        out_shape=[jax.ShapeDtypeStruct((DOFS, slots), F32)] * 2,
        in_specs=[vmem, vmem, hbm, vmem, vmem],
        out_specs=[hbm] * 2,
        scratch_shapes=[
            pltpu.VMEM(extra.shape, F32),
            pltpu.VMEM((BODY, slots), F32),
            pltpu.VMEM((BODY, slots), F32),
            pltpu.SemaphoreType.DMA,
            pltpu.SemaphoreType.DMA((2 * partners // group,)),
        ],
        compiler_params=pltpu.CompilerParams(vmem_limit_bytes=24 * MIB),
        cost_estimate=pl.CostEstimate(flops=4 * 10**9, bytes_accessed=8 * 10**6, transcendentals=0),
        name="body_rows",
    )(recv, flag, extra, off_w, sums_w)


def finish_kernel(one, two, rows_of, lanes_of, base, field, step, _, __, fresh, residual, flat):
    values = jnp.concatenate(
        [one[i : i + 1, :] for i in range(4)] + [two[i : i + 1, :] for i in range(4)], axis=1
    )
    hi, mid = two_pieces(values)
    low = (values - hi.astype(F32) - mid.astype(F32)).astype(BF16)
    spread = lanes_of[...]
    pieces = jnp.concatenate([spread * hi, spread * mid, spread * low], axis=0)
    found = dot(rows_of[...], pieces, NT)
    flat[...] = found[:, 0:128] + found[:, 128:256] + found[:, 256:384]
    for b in range(16):
        at = slice(b * 128, (b + 1) * 128)
        added = flat[pl.ds(b, HEAD, stride=16), :]
        scale = step[:, at]
        left = jnp.where(scale > 0.0, base[:, at] - added, 0.0)
        residual[:, at] = left
        fresh[:, at] = field[:, at] + scale * left


def finish(one, two, rows_of, lanes_of, base, field, step, fresh, residual):
    vmem = pl.BlockSpec(memory_space=pltpu.VMEM)
    there = pl.BlockSpec(memory_space=pl.ANY)
    first = pl.BlockSpec(base.shape, lambda t: (0, 0))
    return pl.pallas_call(
        finish_kernel,
        grid=(1,),
        out_shape=[jax.ShapeDtypeStruct(fresh.shape, F32)] * 2,
        in_specs=[vmem] * 7 + [there] * 2,
        out_specs=[first] * 2,
        scratch_shapes=[pltpu.VMEM((HEAD * 16, 128), F32)],
        input_output_aliases={7: 0, 8: 1},
        compiler_params=pltpu.CompilerParams(vmem_limit_bytes=24 * MIB),
        cost_estimate=pl.CostEstimate(flops=10**9, bytes_accessed=10**6, transcendentals=0),
        name="finish",
    )(one, two, rows_of, lanes_of, base, field, step, fresh, residual)


def per_device(
    iterate,
    rhs,
    material,
    orders,
    new_owner,
    face_send,
    face_recv,
    face_flip,
    stiff_off,
    stiff_diag,
    mass_diag,
):
    count = iterate.shape[1]
    owners = lax.axis_size("grp") * lax.axis_size("dev")
    packed, extra, near_w, far_w, off_w, sums_w, rows_of, lanes_of = pack(
        (
            new_owner.reshape(1, count),
            orders.reshape(1, count),
            face_recv,
            face_flip,
            material,
            stiff_diag,
            mass_diag,
            iterate,
            rhs,
            stiff_off,
        ),
        owners,
    )

    def exchanged(rows):
        return lax.all_to_all(rows, ("grp", "dev"), split_axis=0, concat_axis=0, tiled=True)

    recv = exchanged(packed)
    flag, same = flag_of(recv)
    _, extra = lax.while_loop(
        lambda c: c[0] > 0.5,
        lambda c: (jnp.zeros((), F32), exchanged(c[1])),
        (flag[0, 0], extra),
    )
    base, field, step, one, two = head_rows(recv, same, extra, near_w, far_w, face_send, 16)
    one, two = swapped(one, "dev", 0), swapped(two, "dev", 1)
    fresh, residual = body_rows(recv, same, extra, off_w, sums_w, 32)
    return tuple(finish(one, two, rows_of, lanes_of, base, field, step, fresh, residual))


def solution(mesh):
    both = ("grp", "dev")
    return jax.shard_map(
        per_device,
        mesh=mesh,
        in_specs=(
            P(None, both),
            P(None, both),
            P(None, both),
            P(both),
            P(both, None),
            P(None, both),
            P(None, both),
            P(None, both),
            P(),
            P(),
            P(),
        ),
        out_specs=(P(None, both), P(None, both)),
        check_vma=False,
    )
```

```python
import functools

import jax
import jax.numpy as jnp
from jax import lax
from jax.experimental import pallas as pl
from jax.experimental.pallas import tpu as pltpu
from jax.sharding import PartitionSpec as P

F32 = jnp.float32
BF16 = jnp.bfloat16
CHEBY = 2.0 / (2.0 + 0.2)
DOFS = 216
LIVE = (20, 45, 84, 140, 216)
PADDED = (24, 48, 88, 144, 216)
HEAD = 24
BODY = DOFS - HEAD
CAP = 16
COEFS = 16
NEAR = 88
NEAR_ROWS = CAP + CAP // 2
POOL = 24
POOL_MAX = 2 * CAP
POOL_STRIDE = POOL_MAX + 8
NEAR_W = (len(LIVE) + 3) * HEAD + COEFS
BODY_OFF = sum(n - HEAD for n in PADDED[1:])
NT = (((1,), (1,)), ((), ()))
MIB = 1 << 20
EARLY = 96


def swapped(array, axis, first):
    devices = lax.axis_size(axis)
    lower = range(first, devices - 1, 2)
    return lax.ppermute(array, axis, [p for i in lower for p in ((i, i + 1), (i + 1, i))])


def two_pieces(x):
    hi = x.astype(BF16)
    return hi, (x - hi.astype(F32)).astype(BF16)


def dot(a, b, dims=(((1,), (0,)), ((), ()))):
    return lax.dot_general(a, b, dims, preferred_element_type=F32)


def coefficients(material, order, first_row, overflow):
    c0, c1 = material[0:1], material[1:2]
    live = jnp.zeros(order.shape, jnp.int32)
    for k, n in enumerate(LIVE):
        live = jnp.where(order == k, n, live)
    rows = [c0, c1, live.astype(F32), first_row]
    for c in (c0, c1):
        rows += [jnp.where(order == k, c, 0.0) for k in range(len(LIVE))]
    rows += [jnp.zeros(order.shape, F32), jnp.broadcast_to(overflow, order.shape)]
    return jnp.concatenate(rows, axis=0)


def ranks_of(own_row, sizes, owners):
    chunk = 128
    upper = (
        lax.broadcasted_iota(jnp.int32, (chunk, chunk), 0)
        < lax.broadcasted_iota(jnp.int32, (chunk, chunk), 1)
    )
    sums = jnp.concatenate([upper.astype(F32), jnp.ones((chunk, chunk), F32)], axis=1).astype(BF16)
    carry = jnp.zeros((2 * owners, chunk), F32)
    ranks, firsts = [], []
    for c in range(own_row.shape[1] // chunk):
        here = slice(c * chunk, (c + 1) * chunk)
        named = (
            lax.broadcasted_iota(jnp.int32, (owners, chunk), 0) == own_row[:, here]
        ).astype(F32)
        marks = jnp.concatenate([named, named * sizes[:, here]], axis=0).astype(BF16)
        both = dot(marks, sums)
        earlier = both[:, :chunk] + carry
        carry = carry + both[:, chunk:]
        ranks.append(jnp.sum(named * earlier[:owners], axis=0, keepdims=True))
        firsts.append(jnp.sum(named * earlier[owners:], axis=0, keepdims=True))
    return (jnp.concatenate(v, axis=1) for v in (ranks, firsts)), jnp.max(carry[owners:])


def weights_of(off, divisor):
    lanes = lax.broadcasted_iota(jnp.int32, (HEAD, 128), 1)

    def units(rows, start):
        place = lax.broadcasted_iota(jnp.int32, (rows, 128), 0) + start
        return (place == lax.broadcasted_iota(jnp.int32, (rows, 128), 1)).astype(F32)

    near = [
        jnp.where(lanes < min(n, NEAR), off[k, 0:HEAD, 0:128], 0.0) for k, n in enumerate(LIVE)
    ]
    near += [pltpu.roll(divisor, COEFS, 1)[:HEAD]]
    near += [units(HEAD, 0), units(HEAD, NEAR), units(COEFS, 128 - COEFS)]
    pool = [
        jnp.where(lanes < LIVE[k] - NEAR, off[k, 0:HEAD, NEAR:DOFS], 0.0) for k in (4, 3)
    ]
    body = []
    for k, n in enumerate(PADDED[1:], 1):
        wide = 128 if n < 128 else DOFS
        pad = jnp.zeros((n - HEAD, 256 - wide), F32)
        body.append(jnp.concatenate([off[k, HEAD:n, 0:wide], pad], axis=1))
    at = 128 - 2 * COEFS
    sums = divisor[HEAD:, at : at + COEFS]
    return (jnp.concatenate(v, axis=0) for v in (near, pool, body, [sums]))


def three_passes(w):
    hi, lo = two_pieces(w)
    return jnp.concatenate([hi, lo, hi], axis=1)


def side_by_side(pair, swap):
    both = pair[...]
    there, back = (jnp.concatenate([both[i : i + 1], both[1 - i : 2 - i]], axis=1) for i in (0, 1))
    return jnp.where(swap, back, there)


def odd_device():
    return lax.rem(lax.axis_index("dev"), 2) == 1


def pack_kernel(
    owner_in, orders_in, at_in, flip_in, material_in, diag_in, mass_in, field_in, source_in, off_in,
    out, extra, near_out, far_out, body_out, sums_out, rows_out, lanes_out,
    owner, orders, at, flip, material, diag, mass, field, source, off,
    near_w, far_w, body_w, sums_w, rows_of, lanes_of,
    t0, t1, t2, t3, whole, halves, merged, pool, table,
    coefs_at, slot_index, pool_index, slot_at, pool_at, in_sems, out_sems, index_sems, spill_sem,
):
    count = field.shape[1]
    owners = out.shape[0]
    chunk = 128
    loads = []
    pairs = [
        (owner_in, owner),
        (orders_in, orders),
        (at_in, at),
        (flip_in, flip),
        (material_in, material),
        (diag_in, diag),
        (mass_in, mass),
        (field_in, field),
        (source_in, source),
    ]
    for k, n in enumerate(PADDED):
        part = slice(0, n), slice(0, 128 if n < 128 else DOFS)
        pairs.append((off_in.at[k, part[0], part[1]], off.at[k, part[0], part[1]]))
    for src, dst in pairs:
        loads.append(pltpu.make_async_copy(src, dst, in_sems.at[len(loads)]))
        loads[-1].start()
    sends = []

    def send(src, dst):
        sends.append(pltpu.make_async_copy(src, dst, out_sems.at[len(sends)]))
        sends[-1].start()

    table[...] = jnp.zeros(table.shape, F32)
    pool[...] = jnp.zeros(pool.shape, F32)
    for c in loads[0:2]:
        c.wait()
    own_row, order = owner[...], orders[...]
    sizes = jnp.where(order == 4, 2.0, jnp.where(order == 3, 1.0, 0.0))
    (rank, first_row), largest = ranks_of(own_row, sizes, owners)
    slot_index[...] = own_row * CAP + rank.astype(jnp.int32)
    pool_index[...] = own_row * POOL_STRIDE + first_row.astype(jnp.int32)
    copies = [
        pltpu.make_async_copy(src, dst, index_sems.at[i])
        for i, (src, dst) in enumerate(((pool_index, pool_at), (slot_index, slot_at)))
    ]
    for c in copies:
        c.start()
    overflow = jnp.where(largest > POOL, 1.0, 0.0)
    last = lax.broadcasted_iota(jnp.int32, whole.shape, 1) == 127
    whole[...] = jnp.where(last, overflow, 0.0)

    for c in loads[2:7]:
        c.wait()
    swap = jnp.logical_not(odd_device())
    row = side_by_side(at, swap)
    signs = (1 - 2 * side_by_side(flip, swap)).astype(F32)
    faces = row.shape[1]
    mine = lax.broadcasted_iota(jnp.int32, (HEAD * 16, faces), 0) == row // 128
    rows_of[...] = mine.astype(F32).astype(BF16)
    spot = lax.broadcasted_iota(jnp.int32, (128, faces), 0) == lax.rem(row, 128)
    lanes_of[...] = jnp.where(spot, signs, 0.0).astype(BF16)
    first = 128 - 2 * COEFS + 4
    orders_held = len(LIVE)
    table[first : first + orders_held, 0:DOFS] = diag[...]
    table[first + orders_held : first + 2 * orders_held, 0:DOFS] = mass[...]
    coefs_at[...] = coefficients(material[...], order, first_row, overflow)

    for c in loads[7:]:
        c.wait()
    for c in range(count // chunk):
        here = slice(c * chunk, (c + 1) * chunk)
        top = jnp.where(order[:, here] == 4, field[NEAR + 64 : DOFS, here], source[NEAR : NEAR + 64, here])
        t2[here, :] = jnp.concatenate([field[NEAR : NEAR + 64, here], top], axis=0).T
        t3[here, :] = source[NEAR:DOFS, here].T
    near, far, body, divisor = weights_of(off, table[...].T[:DOFS])
    near_w[...] = three_passes(near)
    far_w[...] = three_passes(far)
    body_w[...] = three_passes(body)
    sums_w[...] = three_passes(divisor)
    for c in copies:
        c.wait()
    for src, dst in (
        (near_w, near_out),
        (far_w, far_out),
        (body_w, body_out),
        (sums_w, sums_out),
        (rows_of, rows_out),
        (lanes_of, lanes_out),
    ):
        send(src, dst)

    def place(row_at, steps, size, also=None):
        def step(g, carry):
            if also is not None:
                also(pl.ds(pl.multiple_of(g * size, size), size))
            for j in range(size):
                i = g * size + j
                row = row_at[0, i]
                for rows, block, ahead in steps:
                    block[pl.ds(row + ahead, 1), :] = rows[pl.ds(i, 1), :]
            return carry

        lax.fori_loop(0, count // size, step, 0)

    def turn(here):
        t0[here, :] = jnp.concatenate(
            [field[0:NEAR, here], source[0:HEAD, here], coefs_at[:, here]], axis=0
        ).T
        middle = source[HEAD:NEAR, here]
        t1[here, :] = jnp.concatenate([middle, middle], axis=0).T

    place(pool_at, [(t2, pool, 0), (t3, pool, 1)], chunk, turn)
    pools = pool.reshape(owners, POOL_STRIDE, 128)
    send(pools.at[:, 0:POOL, :], out.at[:, NEAR_ROWS : NEAR_ROWS + POOL, :])
    spill = pltpu.make_async_copy(pools.at[:, POOL:POOL_MAX, :], extra, spill_sem)

    @pl.when(overflow > 0.5)
    def _():
        spill.start()

    place(slot_at, [(t0, whole, 0), (t1, halves, 0)], 64)
    send(whole.reshape(owners, CAP, 128), out.at[:, 0:CAP, :])
    both = halves[...].reshape(owners, CAP, 128)
    low = lax.broadcasted_iota(jnp.int32, (owners, CAP // 2, 128), 2) < 64
    both = jnp.where(low, both[:, 0 : CAP // 2], both[:, CAP // 2 :])
    merged[...] = both.reshape(merged.shape)
    send(merged.reshape(owners, CAP // 2, 128), out.at[:, CAP:NEAR_ROWS, :])
    for c in sends:
        c.wait()

    @pl.when(overflow > 0.5)
    def _():
        spill.wait()


def pack(operands, owners):
    count = operands[0].shape[1]
    faces = 2 * operands[2].shape[1]
    hbm = pl.BlockSpec(memory_space=pltpu.HBM)
    made = [
        jax.ShapeDtypeStruct((NEAR_W, 384), BF16),
        jax.ShapeDtypeStruct((2 * HEAD, 384), BF16),
        jax.ShapeDtypeStruct((BODY_OFF, 768), BF16),
        jax.ShapeDtypeStruct((BODY, 3 * COEFS), BF16),
        jax.ShapeDtypeStruct((HEAD * 16, faces), BF16),
        jax.ShapeDtypeStruct((128, faces), BF16),
    ]
    return pl.pallas_call(
        pack_kernel,
        out_shape=[
            jax.ShapeDtypeStruct((owners, NEAR_ROWS + POOL, 128), F32),
            jax.ShapeDtypeStruct((owners, POOL_MAX - POOL, 128), F32),
        ]
        + made,
        in_specs=[hbm] * len(operands),
        out_specs=[hbm] * 8,
        scratch_shapes=[pltpu.VMEM(a.shape, a.dtype) for a in list(operands) + made]
        + [pltpu.VMEM((count, 128), F32)] * 4
        + [pltpu.VMEM((owners * CAP, 128), F32)] * 2
        + [
            pltpu.VMEM((owners * CAP // 2, 128), F32),
            pltpu.VMEM((owners * POOL_STRIDE, 128), F32),
            pltpu.VMEM((128, 256), F32),
            pltpu.VMEM((COEFS, count), F32),
            pltpu.VMEM((1, count), jnp.int32),
            pltpu.VMEM((1, count), jnp.int32),
            pltpu.SMEM((1, count), jnp.int32),
            pltpu.SMEM((1, count), jnp.int32),
            pltpu.SemaphoreType.DMA((len(operands) - 1 + len(LIVE),)),
            pltpu.SemaphoreType.DMA((9,)),
            pltpu.SemaphoreType.DMA((2,)),
            pltpu.SemaphoreType.DMA,
        ],
        compiler_params=pltpu.CompilerParams(vmem_limit_bytes=60 * MIB),
        name="pack",
    )(*operands)


def pool_columns(pools, first_row):
    rows, wide = pools.shape
    partners = first_row.shape[1] // CAP
    held = wide // partners
    lane = lax.broadcasted_iota(jnp.int32, (1, 128), 1)
    tiles = []
    for j in range(partners // 8):
        start = j * 8 * held
        tile = start // 128
        at = start % 128 + lane // CAP * held + first_row[:, j * 128 : (j + 1) * 128]
        second = jnp.broadcast_to(at >= 128, (8, 128))
        at = jnp.broadcast_to(jnp.bitwise_and(at, 127), (8, 128))

        def taken(r, tile):
            part = pools[r : r + 8, tile * 128 : (tile + 1) * 128]
            return jnp.take_along_axis(part, at, axis=1, mode="promise_in_bounds")

        tiles.append(
            jnp.concatenate(
                [jnp.where(second, taken(r, tile + 1), taken(r, tile)) for r in range(0, rows, 8)],
                axis=0,
            )
        )
    return jnp.concatenate(tiles, axis=1)


def stacked_pieces(values):
    hi, lo = two_pieces(values)
    return jnp.concatenate([hi, hi, lo], axis=0)


def flag_kernel(recv, flag, same):
    flags = jnp.max(jnp.max(recv[:, 0:8, :], axis=0), axis=0, keepdims=True)
    last = lax.broadcasted_iota(jnp.int32, flags.shape, 1) == 127
    flag[...] = jnp.max(jnp.where(last, flags, 0.0), axis=1, keepdims=True)
    same[...] = flag[...]


def flag_of(recv):
    vmem = pl.BlockSpec(memory_space=pltpu.VMEM)
    return pl.pallas_call(
        flag_kernel,
        out_shape=[jax.ShapeDtypeStruct((1, 1), F32)] * 2,
        in_specs=[vmem],
        out_specs=[vmem] * 2,
        compiler_params=pltpu.CompilerParams(vmem_limit_bytes=16 * MIB),
        name="flag_of",
    )(recv)


def load_overflow(flag, extra, more, sem):
    @pl.when(jnp.max(flag[...]) > 0.5)
    def _():
        copy = pltpu.make_async_copy(extra, more, sem)
        copy.start()
        copy.wait()


def row_pieces(rows):
    hi, lo = two_pieces(rows)
    return jnp.concatenate([hi, hi, lo], axis=1)


def head_kernel(
    recv, flag, extra, near_w, far_w, send,
    base, field, step, one, two, applied_at, more, sem, *, group,
):
    load_overflow(flag, extra, more, sem)
    slots = group * CAP
    for t in range(recv.shape[0] // group):
        at = slice(t * group, (t + 1) * group)
        here = slice(t * slots, (t + 1) * slots)
        near = recv[at, 0:CAP, :].reshape(-1, 128)
        pools = jnp.concatenate([recv[at, NEAR_ROWS:, :], more[at]], axis=1).reshape(-1, 128)
        y = dot(near_w[...], row_pieces(near), NT)
        z = dot(far_w[...], row_pieces(pools), NT)
        diag, x, rhs = (y[(5 + i) * HEAD : (6 + i) * HEAD] for i in range(3))
        coefs = y[8 * HEAD :]
        c0, live = coefs[0:1], coefs[2:3]
        far = pool_columns(z, (coefs[3:4] + 0.5).astype(jnp.int32))
        product = y[0:HEAD]
        for k in range(1, len(LIVE)):
            mine = y[k * HEAD : (k + 1) * HEAD]
            if k >= 3:
                mine = mine + far[(4 - k) * HEAD : (5 - k) * HEAD]
            product = jnp.where(coefs[4 + k : 5 + k] > 0.0, mine, product)
        rows = lax.broadcasted_iota(jnp.int32, (HEAD, slots), 0).astype(F32)
        alive = rows + 0.5 < live
        divisor = jnp.where(alive, diag, 1.0)
        applied = jnp.where(alive, c0 * product + divisor * x, 0.0)
        applied_at[:, here] = applied
        base[:, here] = jnp.where(alive, rhs - applied, 0.0)
        field[:, here] = jnp.where(alive, x, 0.0)
        step[:, here] = jnp.where(alive, CHEBY / divisor, 0.0)

    row = side_by_side(send, odd_device())
    slot = lax.rem(row, 2048)
    lane, block, dof = lax.rem(slot, 128), slot // 128, row // 2048
    rows = lax.broadcasted_iota(jnp.int32, (8, 128), 0)
    for i in range(row.shape[1] // 128):
        part = slice(i * 128, (i + 1) * 128)
        lanes = jnp.broadcast_to(lane[:, part], (8, 128))
        blocks = jnp.broadcast_to(block[:, part], (8, 128))
        dofs = jnp.broadcast_to(dof[:, part], (8, 128))
        total = jnp.zeros((8, 128), F32)
        for d in range(HEAD // 8):
            found = jnp.zeros((8, 128), F32)
            for b in range(applied_at.shape[1] // 128):
                held = applied_at[d * 8 : (d + 1) * 8, b * 128 : (b + 1) * 128]
                taken = jnp.take_along_axis(held, lanes, axis=1, mode="promise_in_bounds")
                found = jnp.where(blocks == b, taken, found)
            total = total + jnp.where(rows + d * 8 == dofs, found, 0.0)
        values = jnp.sum(total, axis=0, keepdims=True)
        if i < 4:
            one[i : i + 1, :] = values
        else:
            two[i - 4 : i - 3, :] = values


def head_rows(recv, flag, extra, near_w, far_w, face_send, group):
    slots = recv.shape[0] * CAP
    vmem = pl.BlockSpec(memory_space=pltpu.VMEM)
    there = pl.BlockSpec(memory_space=pltpu.HBM)
    return pl.pallas_call(
        functools.partial(head_kernel, group=group),
        out_shape=[jax.ShapeDtypeStruct((HEAD, slots), F32)] * 3
        + [jax.ShapeDtypeStruct((4, 128), F32)] * 2,
        in_specs=[vmem] * 2 + [there] + [vmem] * 3,
        out_specs=[vmem] * 5,
        scratch_shapes=[
            pltpu.VMEM((HEAD, slots), F32),
            pltpu.VMEM(extra.shape, F32),
            pltpu.SemaphoreType.DMA,
        ],
        compiler_params=pltpu.CompilerParams(vmem_limit_bytes=24 * MIB),
        cost_estimate=pl.CostEstimate(flops=2 * 10**9, bytes_accessed=4 * 10**6, transcendentals=0),
        name="head_rows",
    )(recv, flag, extra, near_w, far_w, face_send)


def chosen_columns(pools, first_row):
    held = pools.shape[1] * CAP // first_row.shape[1]
    lane = lax.broadcasted_iota(jnp.int32, (1, 128), 1)
    row = lax.broadcasted_iota(jnp.int32, (8 * held, 256), 0)
    fars = []
    for j in range(first_row.shape[1] // 128):
        at = lane // CAP * held + first_row[:, j * 128 : (j + 1) * 128]
        chosen = (row == jnp.concatenate([at, at + 1], axis=1)).astype(F32).astype(BF16)
        hi, lo = two_pieces(pools[:, j * 8 * held : (j + 1) * 8 * held])
        both = dot(jnp.concatenate([hi, lo], axis=0), chosen)
        fars.append(both[0:128] + both[128:256])
    return (
        jnp.concatenate([f[:, i * 128 : (i + 1) * 128] for f in fars], axis=1) for i in range(2)
    )


def unpacked(recv, more, at):
    near = recv[at, 0:CAP, :].reshape(-1, 128).T
    middle = recv[at, CAP:NEAR_ROWS, :]
    turned = pltpu.roll(middle.reshape(-1, 128), 64, 1).reshape(middle.shape)
    middle = jnp.stack([middle, turned], axis=1).reshape(-1, 128).T[0:64]
    pools = jnp.concatenate([recv[at, NEAR_ROWS:, :], more[at]], axis=1).reshape(-1, 128).T
    coefs = near[128 - COEFS :]
    far, far_rhs = chosen_columns(pools, coefs[3:4].astype(jnp.int32))
    slots = near.shape[1]
    rows = lax.broadcasted_iota(jnp.int32, (DOFS, slots), 0).astype(F32)
    alive = rows + 0.5 < coefs[2:3]
    values = jnp.where(alive, jnp.concatenate([near[0:NEAR], far], axis=0), 0.0)
    top = jnp.where(coefs[8:9] > 0.0, far_rhs[0:64], far[64:128])
    rhs = jnp.concatenate([middle, top, far_rhs[64:]], axis=0)
    full = jnp.concatenate([values, jnp.zeros((256 - DOFS, slots), F32)], axis=0)
    return stacked_pieces(full), stacked_pieces(coefs), coefs, values[HEAD:], rhs


def body_step(off_w, sums_w, x, c, coefs, field, rhs):
    y = dot(off_w[...], x)
    c0, live = coefs[0:1], coefs[2:3]
    product = None
    start = BODY_OFF
    for k in range(len(LIVE) - 1, 0, -1):
        size = PADDED[k] - HEAD
        start -= size
        mine = y[start : start + size]
        if product is None:
            product = mine
        else:
            best = jnp.where(coefs[4 + k : 5 + k] > 0.0, mine, product[0:size])
            product = jnp.concatenate([best, product[size:]], axis=0)
    rows = lax.broadcasted_iota(jnp.int32, field.shape, 0).astype(F32) + HEAD
    alive = rows + 0.5 < live
    divisor = jnp.where(alive, dot(sums_w[...], c), 1.0)
    left = jnp.where(alive, rhs - c0 * product - divisor * field, 0.0)
    return field + CHEBY * left / divisor, left


def body_blocks(recv, more, off_w, sums_w, fresh, residual, new, rest, sems, start, stop, group):
    slots = group * CAP
    sends = []
    ready = unpacked(recv, more, slice(start, start + group))
    for p in range(start, stop, group):
        now = ready
        if p + group < stop:
            ready = unpacked(recv, more, slice(p + group, p + 2 * group))
        here = slice((p - start) * CAP, (p - start) * CAP + slots)
        there = slice(p * CAP, p * CAP + slots)
        new[:, here], rest[:, here] = body_step(off_w, sums_w, *now)
        for src, dst in ((new, fresh), (rest, residual)):
            sends.append(
                pltpu.make_async_copy(
                    src.at[:, here], dst.at[HEAD:DOFS, there], sems.at[len(sends)]
                )
            )
            sends[-1].start()
    return sends


def early_kernel(recv, flag, extra, off_w, sums_w, new, rest, more, sem, *, stop, group):
    more[...] = jnp.zeros(more.shape, F32)
    load_overflow(flag, extra, more, sem)
    slots = group * CAP
    ready = unpacked(recv, more, slice(0, group))
    for p in range(0, stop, group):
        now = ready
        if p + group < stop:
            ready = unpacked(recv, more, slice(p + group, p + 2 * group))
        here = slice(p * CAP, p * CAP + slots)
        new[:, here], rest[:, here] = body_step(off_w, sums_w, *now)


def late_kernel(
    one, two, rows_of, lanes_of, base, field, step, recv, flag, extra, off_w, sums_w, early, before,
    fresh, residual, flat, top, bottom, more, new, rest, sem, top_sems, sems, *, start, group,
):
    done = [
        pltpu.make_async_copy(
            src, dst.at[HEAD:DOFS, 0 : start * CAP], top_sems.at[2 + i]
        )
        for i, (src, dst) in enumerate(((early, fresh), (before, residual)))
    ]
    for c in done:
        c.start()
    more[...] = jnp.zeros(more.shape, F32)
    load_overflow(flag, extra, more, sem)
    values = jnp.concatenate(
        [one[i : i + 1, :] for i in range(4)] + [two[i : i + 1, :] for i in range(4)], axis=1
    )
    hi, mid = two_pieces(values)
    low = (values - hi.astype(F32) - mid.astype(F32)).astype(BF16)
    spread = lanes_of[...]
    pieces = jnp.concatenate([spread * hi, spread * mid, spread * low], axis=0)
    found = dot(rows_of[...], pieces, NT)
    flat[...] = found[:, 0:128] + found[:, 128:256] + found[:, 256:384]
    blocks = base.shape[1] // 128
    for b in range(blocks):
        at = slice(b * 128, (b + 1) * 128)
        added = flat[pl.ds(b, HEAD, stride=blocks), :]
        scale = step[:, at]
        left = jnp.where(scale > 0.0, base[:, at] - added, 0.0)
        bottom[:, at] = left
        top[:, at] = field[:, at] + scale * left
    sends = [
        pltpu.make_async_copy(src, dst.at[0:HEAD, :], top_sems.at[i])
        for i, (src, dst) in enumerate(((top, fresh), (bottom, residual)))
    ]
    for c in sends:
        c.start()
    sends += body_blocks(
        recv, more, off_w, sums_w, fresh, residual, new, rest, sems, start, recv.shape[0], group
    )
    for c in done + sends:
        c.wait()


def body_scratch(extra, partners, group):
    return [
        pltpu.VMEM(extra.shape, F32),
        pltpu.VMEM((BODY, partners * CAP), F32),
        pltpu.VMEM((BODY, partners * CAP), F32),
        pltpu.SemaphoreType.DMA,
    ], [pltpu.SemaphoreType.DMA((2 * partners // group,))]


def early_rows(recv, flag, extra, off_w, sums_w, stop, group):
    vmem = pl.BlockSpec(memory_space=pltpu.VMEM)
    hbm = pl.BlockSpec(memory_space=pltpu.HBM)
    return pl.pallas_call(
        functools.partial(early_kernel, stop=stop, group=group),
        out_shape=[jax.ShapeDtypeStruct((BODY, stop * CAP), F32)] * 2,
        in_specs=[vmem, vmem, hbm, vmem, vmem],
        out_specs=[vmem] * 2,
        scratch_shapes=[pltpu.VMEM(extra.shape, F32), pltpu.SemaphoreType.DMA],
        compiler_params=pltpu.CompilerParams(vmem_limit_bytes=24 * MIB),
        cost_estimate=pl.CostEstimate(flops=4 * 10**9, bytes_accessed=8 * 10**6, transcendentals=0),
        name="early_rows",
    )(recv, flag, extra, off_w, sums_w)


def late_rows(faces, body, early, before, start, group):
    recv, _, extra = body[:3]
    base = faces[4]
    vmem = pl.BlockSpec(memory_space=pltpu.VMEM)
    hbm = pl.BlockSpec(memory_space=pltpu.HBM)
    held, sems = body_scratch(extra, recv.shape[0] - start, group)
    return pl.pallas_call(
        functools.partial(late_kernel, start=start, group=group),
        out_shape=[jax.ShapeDtypeStruct((DOFS, recv.shape[0] * CAP), F32)] * 2,
        in_specs=[vmem] * 9 + [hbm] + [vmem] * 4,
        out_specs=[hbm] * 2,
        scratch_shapes=[pltpu.VMEM((HEAD * 16, 128), F32)]
        + [pltpu.VMEM(base.shape, F32)] * 2
        + held
        + [pltpu.SemaphoreType.DMA((4,))]
        + sems,
        compiler_params=pltpu.CompilerParams(vmem_limit_bytes=24 * MIB),
        cost_estimate=pl.CostEstimate(flops=4 * 10**9, bytes_accessed=8 * 10**6, transcendentals=0),
        name="late_rows",
    )(*faces, *body, early, before)


def per_device(
    iterate,
    rhs,
    material,
    orders,
    new_owner,
    face_send,
    face_recv,
    face_flip,
    stiff_off,
    stiff_diag,
    mass_diag,
):
    count = iterate.shape[1]
    owners = lax.axis_size("grp") * lax.axis_size("dev")
    packed, extra, near_w, far_w, off_w, sums_w, rows_of, lanes_of = pack(
        (
            new_owner.reshape(1, count),
            orders.reshape(1, count),
            face_recv,
            face_flip,
            material,
            stiff_diag,
            mass_diag,
            iterate,
            rhs,
            stiff_off,
        ),
        owners,
    )

    def exchanged(rows):
        return lax.all_to_all(rows, ("grp", "dev"), split_axis=0, concat_axis=0, tiled=True)

    recv = exchanged(packed)
    flag, same = flag_of(recv)
    _, extra = lax.while_loop(
        lambda c: c[0] > 0.5,
        lambda c: (jnp.zeros((), F32), exchanged(c[1])),
        (flag[0, 0], extra),
    )
    base, field, step, one, two = head_rows(recv, same, extra, near_w, far_w, face_send, 16)
    one, two = swapped(one, "dev", 0), swapped(two, "dev", 1)
    body = (recv, same, extra, off_w, sums_w)
    early, before = early_rows(*body, EARLY, 32)
    faces = (one, two, rows_of, lanes_of, base, field, step)
    return tuple(late_rows(faces, body, early, before, EARLY, 32))


def solution(mesh):
    both = ("grp", "dev")
    return jax.shard_map(
        per_device,
        mesh=mesh,
        in_specs=(
            P(None, both),
            P(None, both),
            P(None, both),
            P(both),
            P(both, None),
            P(None, both),
            P(None, both),
            P(None, both),
            P(),
            P(),
            P(),
        ),
        out_specs=(P(None, both), P(None, both)),
        check_vma=False,
    )
```
